1024 devices in a mesh: table: 16 (over x, core), rep: 64 (over z, y).
Axes of the slice: x: 8, y: 8, z: 8, core: 2. Of those that a mesh axis runs over, the one named last changes fastest.
Arguments:
- tokens: bfloat16 [131072, 512], P(('table', 'rep')), may hold values from -6 to 6
- cotangent: bfloat16 [131072, 512], P(('table', 'rep')), may hold values from -6 to 6
- hist_len: int32 [2048], P(('table', 'rep')), may hold values from 16 to 64, as said below
- item_owner: int32 [131072, 1], P(('table', 'rep')), may hold values from 0 to 15; in each aligned block of 128 rows (0 to 127, 128 to 255, ...) at most 16 rows name the same one
- item_slot: int32 [131072], P(('table', 'rep')), may hold values from 0 to 511
- w_in: bfloat16 [512, 2048], replicated, may hold values from -0.25 to 0.25
- w_out: bfloat16 [512, 512], replicated, may hold values from -0.25 to 0.25
Outputs:
- touched_grad: float32 [8192, 512], P(('table', 'rep'))
- w_in_grad: float32 [512, 2048], P('table', 'rep')
- w_out_grad: float32 [512, 512], P('table', 'rep')
The draws below stay inside these ranges and needn't reach their ends.
Inputs may be any that keep to these rules, and one draw needn't show every extreme that they name: `hist_len`: histories are ragged; one of length 64 in every draw. `item_owner`: the rows of one device name any one owner at most 16 times; some owner exactly 16 times in some or all devices.
All inputs are finite; a program needn't handle non-finite values.
Results may differ from the reference program's by a relative error of at most 0.023.
Values may be sent and summed in bfloat16 or wider, within the bound.
A program may use at most 32 MiB of HBM per device.

```python
import math
import jax
import jax.numpy as jnp
import numpy as np
from jax import lax

D = 512
HEADS = 4
SEQ = 64
TOK_DEV = 128
HISTS = 2048
TOKENS = 131072
HV = 512
QKUV = 2048
CAP = 16
SLOTS = 512
UNIQ = 8192
N_TABLE = 16


def draw_hist_len(key, part):
    key = jax.random.fold_in(key, 11)
    lengths = jax.random.randint(key, (HISTS,), SEQ // 4, SEQ + 1)
    return lengths.at[0].set(SEQ).astype(jnp.int32)


def plant(array, own_key, low, top_value):
    longest = array.shape.index(max(array.shape))
    spots = []
    for shift in (0, 1):
        where = [jax.random.randint(jax.random.fold_in(own_key, axis), (), 0, length) for axis, length in enumerate(array.shape)]
        where[longest] = (where[longest] + shift) % array.shape[longest]
        spots.append(tuple(where))
    return array.at[spots[0]].set(low).at[spots[1]].set(top_value)


def level_of(stream_key, shape, pieces, smallest, largest):
    def one(position, blocks):
        heights = jax.random.uniform(jax.random.fold_in(jax.random.fold_in(stream_key, 6), position), (blocks,), jnp.float32, smallest / len(pieces), largest / len(pieces))
        return jnp.repeat(jnp.exp(heights), shape[position] // blocks).reshape((-1,) + (1,) * (len(shape) - position - 1))

    factor_of = one(*pieces[0])
    for cut in pieces[1:]:
        factor_of = factor_of * one(*cut)
    return factor_of


def routed_block(key, own, number, rows, amount, top, reach, lean):
    order = jax.random.permutation(key, amount)
    packed, ordinary = shares(amount, rows * top, reach, lean, True), shares(amount, rows * top, reach, lean, False)
    places = jnp.arange(amount)

    def named(sizes, rotation):
        used = int((sizes > 0).sum())
        fixed = max(1, used // 4)
        shifted = fixed + (places - fixed + rotation * (used - fixed)) % max(1, amount - fixed)
        return jnp.zeros((amount,), jnp.int32).at[order[jnp.where(places < fixed, places, shifted)]].set(jnp.asarray(sizes, jnp.int32))

    sizes = jnp.where(number % 4 == 0, named(packed, number // 4), named(ordinary, number - number // 4 - 1))
    mixed = jax.random.permutation(jax.random.fold_in(own, 3), amount)
    source_of, sink = mixed[0:amount // 2 * 2:2], mixed[1:amount // 2 * 2:2]
    margin = jnp.minimum(sizes[source_of] - 1, reach - sizes[sink]) // 2
    margin = jnp.where((source_of == order[0]) | (sink == order[0]) | (sizes[sink] == 0), 0, jnp.maximum(margin, 0))
    shifted = jax.random.randint(jax.random.fold_in(own, 4), (amount // 2,), 0, 1 << 20) % (margin + 1)
    sizes = sizes.at[source_of].add(-shifted).at[sink].add(shifted)
    members = jnp.searchsorted(jnp.cumsum(sizes), jnp.arange(rows * top), side="right").astype(jnp.int32)
    listing = members.reshape(top, rows).T
    listing = listing[jax.random.permutation(jax.random.fold_in(own, 1), rows)]
    rotation = jax.random.randint(jax.random.fold_in(own, 2), (rows, 1), 0, top)
    return jnp.take_along_axis(listing, (jnp.arange(top)[None, :] + rotation) % top, axis=1)


def shares(amount, total, reach, skew, full):
    weights = [(1 << 20) // math.isqrt(standing ** skew) + 1 for standing in range(1, amount + 1)]
    largest = reach if full else min(reach, max(-(-total // amount), total * weights[0] // sum(weights)))
    least = 1 if total - largest >= amount - 1 else 0
    counts, surplus = [largest] + [least] * (amount - 1), total - largest - least * (amount - 1)
    while surplus > 0:
        free = [i for i in range(1, amount) if counts[i] < largest] or [i for i in range(1, amount) if counts[i] < reach]
        whole, left = sum([weights[i] for i in free]), surplus
        for i in free:
            more = min(reach - counts[i], max(1, left * weights[i] // whole), surplus)
            counts[i] = counts[i] + more
            surplus = surplus - more
    return np.array(counts)


def bell_draw(own_key, extent, spread, reach, cuts=(), kind=jnp.bfloat16):
    array = jax.random.normal(own_key, extent, jnp.float32) * spread
    if len(cuts) > 0:
        array = level_of(own_key, extent, cuts, -0.22, 0.18) * array
    return jnp.clip(array, min=-reach, max=reach).astype(kind)


def setup_inputs(seed: int = 0) -> dict:
    key_of = jax.random.split(jax.random.key(seed), 8)
    tokens = bell_draw(key_of[0], (TOKENS, D), 1.0, 6.0, ((0, 1024),))
    cotangent = bell_draw(key_of[1], (TOKENS, D), 1.0, 6.0, ((0, 1024),))
    hist_len = draw_hist_len(jax.random.fold_in(key_of[7], 71), 0)
    item_owner_keys = jax.random.split(jax.random.fold_in(key_of[3], 1), TOKENS // TOK_DEV)
    item_owner_turns = jax.random.permutation(jax.random.fold_in(key_of[3], 3), TOKENS // TOK_DEV)
    item_owner = jax.vmap(lambda own, number: routed_block(jax.random.fold_in(key_of[3], 2), own, number, TOK_DEV, N_TABLE, 1, CAP, 2))(item_owner_keys, item_owner_turns).reshape((TOKENS, 1))
    item_slot = plant(jax.random.randint(key_of[4], (TOKENS,), 0, SLOTS), jax.random.fold_in(key_of[4], 1), 0, SLOTS - 1).astype(jnp.int32)
    w_in = bell_draw(key_of[5], (D, QKUV), D ** -0.5, 0.25)
    w_out = bell_draw(key_of[6], (HV, D), HV ** -0.5, 0.25)
    return {"tokens": tokens, "cotangent": cotangent, "hist_len": hist_len, "item_owner": item_owner, "item_slot": item_slot, "w_in": w_in, "w_out": w_out}


def norm_rows(values):
    middle = lax.optimization_barrier(jnp.mean(values, axis=-1, keepdims=True))
    centered = values - middle
    inverse = lax.rsqrt(lax.optimization_barrier(jnp.mean(centered * centered, axis=-1, keepdims=True)) + 1e-06)
    return (centered * inverse, inverse)

def norm_back(upstream, normed, inverse):
    first = lax.optimization_barrier(jnp.mean(upstream, axis=-1, keepdims=True))
    second = lax.optimization_barrier(jnp.mean(upstream * normed, axis=-1, keepdims=True))
    return inverse * (upstream - first - normed * second)

def silu_grad(values):
    sigma = jax.nn.sigmoid(values)
    return sigma * (1.0 + values * (1.0 - sigma))

def layer_back(tokens, cotangent, lengths, w_in, w_out):
    batch, slots, width = tokens.shape
    heads = HEADS
    head_size = w_out.shape[0] // heads
    feats = heads * head_size
    score_scale = 1.0 / math.sqrt(head_size)
    places = jnp.arange(slots, dtype=jnp.int32)
    valid = places[None, :] < lengths[:, None]
    causal = places[:, None] >= places[None, :]
    keep = (causal[None, :, :] & valid[:, None, :])[:, None, :, :]
    normed, inv_tok = norm_rows(tokens.astype(jnp.float32))
    normed_b = normed.astype(jnp.bfloat16)
    flat_norm = normed_b.reshape(-1, width)
    pre = jnp.dot(flat_norm, w_in, preferred_element_type=jnp.float32)
    hidden = jax.nn.silu(pre).astype(jnp.bfloat16).reshape(batch, slots, 4, heads, head_size)
    gate_u = hidden[:, :, 0]
    vals = hidden[:, :, 1]
    query = hidden[:, :, 2]
    keys = hidden[:, :, 3]
    score = jnp.einsum('bihd,bjhd->bhij', query.astype(jnp.float32), keys.astype(jnp.float32)) * score_scale
    att = jnp.where(keep, jax.nn.silu(score) / slots, 0.0).astype(jnp.bfloat16)
    mixed = jnp.einsum('bhij,bjhd->bihd', att.astype(jnp.float32), vals.astype(jnp.float32)).reshape(batch, slots, feats)
    on_mix, inv_mix = norm_rows(mixed)
    gate_f = gate_u.reshape(batch, slots, feats).astype(jnp.float32)
    gated = (on_mix * gate_f).astype(jnp.bfloat16)
    err = jnp.where(valid[:, :, None], cotangent, jnp.zeros_like(cotangent))
    flat_err = err.reshape(-1, width)
    part_out = jnp.dot(gated.reshape(-1, feats).T, flat_err, preferred_element_type=jnp.float32)
    dgate = jnp.dot(flat_err, w_out.T, preferred_element_type=jnp.float32).reshape(batch, slots, feats)
    grad_u = dgate * on_mix
    dmix = norm_back(dgate * gate_f, on_mix, inv_mix).astype(jnp.bfloat16)
    dmix_h = dmix.reshape(batch, slots, heads, head_size).astype(jnp.float32)
    datt = jnp.einsum('bihd,bjhd->bhij', dmix_h, vals.astype(jnp.float32))
    dscore = jnp.where(keep, datt * silu_grad(score) / slots, 0.0).astype(jnp.bfloat16).astype(jnp.float32)
    grad_v = jnp.einsum('bhij,bihd->bjhd', att.astype(jnp.float32), dmix_h)
    grad_q = jnp.einsum('bhij,bjhd->bihd', dscore, keys.astype(jnp.float32)) * score_scale
    grad_k = jnp.einsum('bhij,bihd->bjhd', dscore, query.astype(jnp.float32)) * score_scale
    grad_h = jnp.concatenate([grad_u, grad_v.reshape(batch, slots, feats), grad_q.reshape(batch, slots, feats), grad_k.reshape(batch, slots, feats)], axis=-1)
    dpre = (grad_h.reshape(-1, 4 * feats) * silu_grad(pre)).astype(jnp.bfloat16)
    part_in = jnp.dot(flat_norm.T, dpre, preferred_element_type=jnp.float32)
    dnorm = jnp.dot(dpre, w_in.T, preferred_element_type=jnp.float32).reshape(batch, slots, width)
    rows = (err.astype(jnp.float32) + norm_back(dnorm, normed, inv_tok)).astype(jnp.bfloat16)
    return (rows.reshape(-1, width), part_in, part_out)

def reference(tokens, cotangent, hist_len, item_owner, item_slot, w_in, w_out):
    blocks = 32
    inputs = tokens.reshape(blocks, -1, SEQ, D)
    grads = cotangent.reshape(blocks, -1, SEQ, D)
    lengths = hist_len.reshape(blocks, -1)

    def step(carry, piece):
        rows, part_in, part_out = layer_back(piece[0], piece[1], piece[2], w_in, w_out)
        return ((carry[0] + part_in, carry[1] + part_out), rows)
    start = (jnp.zeros((D, QKUV), jnp.float32), jnp.zeros((HV, D), jnp.float32))
    totals, rows = lax.scan(step, start, (inputs, grads, lengths))
    scale = 1.0 / math.sqrt(TOKENS)
    target = item_owner[:, 0].astype(jnp.int32) * SLOTS + item_slot.astype(jnp.int32)
    touched = jnp.zeros((UNIQ, D), jnp.float32).at[target].add(rows.reshape(-1, D).astype(jnp.float32))
    return (touched, totals[0] * scale, totals[1] * scale)
```

```python
import math

import jax
import jax.numpy as jnp
from jax import lax
from jax.experimental import pallas as pl
from jax.experimental.pallas import tpu as pltpu
from jax.sharding import PartitionSpec as P

D = 512
HEADS = 4
DH = 128
SLOTS_H = 64
TOK = 128
F32 = jnp.float32
BF16 = jnp.bfloat16
MESH = pl.DeviceIdType.MESH
NT = (((1,), (1,)), ((), ()))
TN = (((0,), (0,)), ((), ()))


def mm(a, b, dims=(((1,), (0,)), ((), ()))):
    return lax.dot_general(a, b, dims, preferred_element_type=F32)


def norm_rows(values):
    middle = jnp.mean(values, axis=-1, keepdims=True)
    centered = values - middle
    inverse = lax.rsqrt(jnp.mean(centered * centered, axis=-1, keepdims=True) + 1e-06)
    return centered * inverse, inverse


def norm_back(upstream, normed, inverse):
    first = jnp.mean(upstream, axis=-1, keepdims=True)
    second = jnp.mean(upstream * normed, axis=-1, keepdims=True)
    return inverse * (upstream - first - normed * second)


def sigmoid(values):
    return 0.5 * jnp.tanh(0.5 * values) + 0.5


def iota(shape, dim):
    return lax.broadcasted_iota(jnp.int32, shape, dim)


def cells(block):
    lo = block[:, :128].reshape(64, 8, 128)
    hi = block[:, 128:].reshape(64, 8, 128)
    return jnp.concatenate([lo, hi], axis=1).reshape(8, 8, 16, 128).astype(BF16)


def kernel(
    len_ref, tok_ref, cot_ref, own_ref, slot_ref, w_in_hbm, w_out_hbm,
    touched_ref, gin_ref, gout_ref,
    w_in, w_out, sgrad, hid, d2, nb2, gt2, er2, nbf, gtf,
    out_rows, in_rows, a_own, a_recv, b_own, b_recv,
    t1_own, t1_recv, t2_own, t2_recv,
    a2_own, a2_recv, b2_own, b2_recv, t3_own, t3_recv, t4_own, t4_recv,
    x_own, x_recv, flip,
    w_sem, pair_s, pair_r, row_s, row_r, a_s, a_r, b_s, b_r,
    t1_s, t1_r, t2_s, t2_r, a2_s, a2_r, b2_s, b2_r, t3_s, t3_r, t4_s, t4_r, x_s, x_r,
):
    t = lax.axis_index("table")
    r = lax.axis_index("rep")
    x, core = lax.div(t, 2), lax.rem(t, 2)
    z, y = lax.div(r, 8), lax.rem(r, 8)

    def turn(base, k, n=8):
        return lax.rem(base + (k + n), n)

    def at_z(k):
        return (t, turn(z, k) * 8 + y)

    def at_y(k):
        return (t, z * 8 + turn(y, k))

    def at_t(k):
        return (turn(t, k, 16), r)

    def at_x(k):
        return (turn(x, k) * 2 + core, r)

    mate = (x * 2 + (1 - core), r)
    sent = []

    def push(src, dst, ssem, rsem, where):
        copy = pltpu.make_async_remote_copy(
            src_ref=src, dst_ref=dst, send_sem=ssem, recv_sem=rsem,
            device_id=where, device_id_type=MESH,
        )
        copy.start()
        sent.append(copy)
        return copy

    barrier = pltpu.get_barrier_semaphore()
    partners = [at_z(k) for k in range(1, 8)] + [at_y(k) for k in range(1, 8)]
    partners += [at_t(k) for k in range(1, 16)]
    for where in partners:
        pl.semaphore_signal(barrier, inc=1, device_id=where, device_id_type=MESH)

    loads = []
    for b in range(4):
        cols = pl.ds(b * 512, 512)
        loads.append(pltpu.make_async_copy(w_in_hbm.at[:, cols], w_in.at[:, cols], w_sem.at[b]))
    loads.append(pltpu.make_async_copy(w_out_hbm, w_out, w_sem.at[4]))
    for load in loads:
        load.start()

    len0, len1 = len_ref[0], len_ref[1]
    ri, ci = iota((TOK, TOK), 0), iota((TOK, TOK), 1)
    same = (ri < SLOTS_H) == (ci < SLOTS_H)
    limit = jnp.where(ci < SLOTS_H, len0, len1 + SLOTS_H)
    keep = same & (ci <= ri) & (ci < limit)
    rows_i = iota((TOK, D), 0)
    valid = rows_i < jnp.where(rows_i < SLOTS_H, len0, len1 + SLOTS_H)

    normed, inv_tok = norm_rows(tok_ref[...].astype(F32))
    nb = normed.astype(BF16)
    pi, pj = iota((D, D), 0), iota((D, D), 1)
    source = ((pj // 32) % 8) * 64 + (pj // 256) * 32 + pj % 32
    perm = jnp.where(pi == source, 1.0, 0.0).astype(BF16)
    nbp = mm(nb, perm).astype(BF16)
    nbf[0] = nbp[:, :256]
    nbf[1] = nbp[:, 256:]
    nb2[0:TOK, :] = nbf[core]
    err = jnp.where(valid, cot_ref[...], jnp.zeros((TOK, D), BF16))
    er2[0:TOK, :] = err
    for b in range(4):
        cols = pl.ds(b * 512, 512)
        loads[b].wait()
        pre = mm(nb, w_in[:, cols])
        sig = sigmoid(pre)
        hid[:, cols] = (pre * sig).astype(BF16)
        sgrad[:, cols] = sig * (1.0 + pre * (1.0 - sig))
    pl.semaphore_wait(barrier, len(partners))
    pair = [
        push(er2.at[pl.ds(0, TOK)], er2.at[pl.ds(TOK, TOK)], pair_s.at[0], pair_r.at[0], mate),
        push(nbf.at[1 - core], nb2.at[pl.ds(TOK, TOK)], pair_s.at[1], pair_r.at[1], mate),
    ]
    score_scale = 1.0 / math.sqrt(DH)
    atts, slopes, mixes = [], [], []
    for h in range(HEADS):
        query = hid[:, 1024 + h * DH:1024 + (h + 1) * DH]
        keys = hid[:, 1536 + h * DH:1536 + (h + 1) * DH]
        vals = hid[:, 512 + h * DH:512 + (h + 1) * DH]
        score = mm(query, keys, NT) * score_scale
        sig = sigmoid(score)
        att = jnp.where(keep, score * sig * (1.0 / SLOTS_H), 0.0).astype(BF16)
        slopes.append(jnp.where(keep, sig * (1.0 + score * (1.0 - sig)) * (1.0 / SLOTS_H), 0.0))
        atts.append(att)
        mixes.append(mm(att, vals))
    on_mix, inv_mix = norm_rows(jnp.concatenate(mixes, axis=1))
    gate = hid[:, 0:512].astype(F32)
    gated = (on_mix * gate).astype(BF16)
    gtp = mm(gated, perm).astype(BF16)
    gtf[0] = gtp[:, :256]
    gtf[1] = gtp[:, 256:]
    gt2[0:TOK, :] = gtf[core]
    pair.append(push(gtf.at[1 - core], gt2.at[pl.ds(TOK, TOK)], pair_s.at[2], pair_r.at[2], mate))

    loads[4].wait()
    dgate = mm(err, w_out[...], NT)

    def give(b, value):
        cols = pl.ds(b * 512, 512)
        d2[0:TOK, cols] = (value * sgrad[:, cols]).astype(BF16)
        pair.append(push(
            d2.at[pl.ds(0, TOK), cols], d2.at[pl.ds(TOK, TOK), cols],
            pair_s.at[3 + b], pair_r.at[3 + b], mate,
        ))

    give(0, dgate * on_mix)
    dmix = norm_back(dgate * gate, on_mix, inv_mix).astype(BF16)
    gv, gq, gk = [], [], []
    for h in range(HEADS):
        query = hid[:, 1024 + h * DH:1024 + (h + 1) * DH]
        keys = hid[:, 1536 + h * DH:1536 + (h + 1) * DH]
        vals = hid[:, 512 + h * DH:512 + (h + 1) * DH]
        part = dmix[:, h * DH:(h + 1) * DH]
        dscore = (mm(part, vals, NT) * slopes[h]).astype(BF16)
        gv.append(mm(atts[h], part, TN))
        gq.append(mm(dscore, keys) * score_scale)
        gk.append(mm(dscore, query, TN) * score_scale)
    give(1, jnp.concatenate(gv, axis=1))
    give(2, jnp.concatenate(gq, axis=1))
    give(3, jnp.concatenate(gk, axis=1))
    dnorm = mm(d2[0:TOK, 0:512], w_in[:, 0:512], NT)
    for b in range(1, 4):
        dnorm += mm(d2[0:TOK, b * 512:(b + 1) * 512], w_in[:, b * 512:(b + 1) * 512], NT)
    rows = (err.astype(F32) + norm_back(dnorm, normed, inv_tok)).astype(BF16)

    owner = own_ref[...]
    slot = slot_ref[...]
    mine = iota((16, TOK), 0) == owner
    hot = jnp.where(mine, 1.0, 0.0)
    before = jnp.where(ri < ci, 1.0, 0.0).astype(BF16)
    earlier = mm(hot.astype(BF16), before)
    placed = jnp.sum(earlier * hot, axis=0, keepdims=True)
    key = owner.astype(F32) * 16.0 + placed
    pick = jnp.where(iota((256, TOK), 0).astype(F32) == key, 1.0, 0.0)
    packed = mm(pick.astype(BF16), rows).astype(BF16)
    s_z = jnp.sum(pick * (slot // 64).astype(F32), axis=1, keepdims=True)
    s_y = jnp.sum(pick * ((slot // 8) % 8).astype(F32), axis=1, keepdims=True)
    s_i = jnp.sum(pick * (slot % 8).astype(F32), axis=1, keepdims=True)
    lane = iota((256, 128), 1)
    tail = jnp.where(lane == 0, s_z, jnp.where(lane == 1, s_y, jnp.where(lane == 2, s_i, 0.0)))
    out_rows[:, :, 0:512] = packed.reshape(16, 16, 512)
    out_rows[:, :, 512:640] = tail.astype(BF16).reshape(16, 16, 128)
    in_rows[0] = out_rows[t]
    row_copies = []
    for k in (8, 7, 9, 6, 10, 5, 11, 4, 12, 3, 13, 2, 14, 1, 15):
        row_copies.append(push(
            out_rows.at[turn(t, k, 16)], in_rows.at[k], row_s.at[k], row_r.at[k], at_t(k)
        ))

    for copy in pair[:3]:
        copy.wait_recv()
    a_own[:, :, 32:48, :] = cells(mm(er2[...], gt2[...], TN))
    for copy in pair[3:]:
        copy.wait_recv()

    def block(k):
        d = turn(z, k)
        cols = pl.ds(pl.multiple_of(d * 256, 256), 256)
        part = mm(d2[:, cols], nb2[...], TN)
        a_own[d, :, 0:32, :] = part[:, :128].reshape(8, 32, 128).astype(BF16)
        b_own[:, d] = part[:, 128:].reshape(8, 32, 128).astype(BF16)

    def ring_step(own, recv, ssem, rsem, base, where, step, previous):
        made = []
        for up in (True, False):
            if not up and step == 3:
                continue
            k = 4 - step if up else step - 3
            slot_no = step if up else 4 + step
            d = turn(base, k)
            if step > 0:
                previous[0 if up else 1].wait_recv()
                own[d] = (own[d].astype(F32) + recv[slot_no - 1].astype(F32)).astype(BF16)
            made.append(push(
                own.at[d], recv.at[slot_no], ssem.at[slot_no], rsem.at[slot_no], where(1 if up else -1)
            ))
        return made if len(made) == 2 else [made[0], previous[1]]

    def ring_end(own, recv, base, previous):
        previous[0].wait_recv()
        previous[1].wait_recv()
        return own[base].astype(F32) + recv[3].astype(F32) + recv[6].astype(F32)

    block(4)
    block(-3)
    ca = ring_step(a_own, a_recv, a_s, a_r, z, at_z, 0, None)
    for k in (3, -2, 2, -1, 1, 0):
        block(k)
    cb = ring_step(b_own, b_recv, b_s, b_r, y, at_y, 0, None)
    ca = ring_step(a_own, a_recv, a_s, a_r, z, at_z, 1, ca)
    cb = ring_step(b_own, b_recv, b_s, b_r, y, at_y, 1, cb)

    for copy in row_copies:
        copy.wait_recv()
    arrived = in_rows[...].reshape(256, 640)
    numbers = arrived[:, 512:640].astype(F32)
    by_z = jnp.where(lane == 0, 64.0, jnp.where(lane == 1, 8.0, jnp.where(lane == 2, 1.0, 0.0)))
    by_y = jnp.where(lane == 0, 8.0, jnp.where(lane == 1, 64.0, jnp.where(lane == 2, 1.0, 0.0)))
    line = iota((256, 512), 1).astype(F32)
    hot_z = jnp.where(line == jnp.sum(numbers * by_z, axis=1, keepdims=True), 1.0, 0.0)
    hot_y = jnp.where(line == jnp.sum(numbers * by_y, axis=1, keepdims=True), 1.0, 0.0)
    t1_own[...] = cells(mm(hot_z.astype(BF16), arrived[:, 0:256], TN))
    t2_own[...] = cells(mm(hot_y.astype(BF16), arrived[:, 256:512], TN))
    ct = []
    for k in (4, 3, 5, 2, 6, 1, 7):
        ct.append(push(t1_own.at[turn(z, k)], t1_recv.at[k], t1_s.at[k], t1_r.at[k], at_z(k)))
        ct.append(push(t2_own.at[turn(y, k)], t2_recv.at[k], t2_s.at[k], t2_r.at[k], at_y(k)))

    for step in (2, 3):
        ca = ring_step(a_own, a_recv, a_s, a_r, z, at_z, step, ca)
        cb = ring_step(b_own, b_recv, b_s, b_r, y, at_y, step, cb)
    a2_own[...] = ring_end(a_own, a_recv, z, ca).astype(BF16)
    c2 = []
    for k in (4, 3, 5, 2, 6, 1, 7):
        c2.append(push(a2_own.at[turn(y, k)], a2_recv.at[k], a2_s.at[k], a2_r.at[k], at_y(k)))
    b2_own[...] = ring_end(b_own, b_recv, y, cb).astype(BF16)
    for k in (4, 3, 5, 2, 6, 1, 7):
        c2.append(push(b2_own.at[turn(z, k)], b2_recv.at[k], b2_s.at[k], b2_r.at[k], at_z(k)))

    for copy in ct:
        copy.wait_recv()

    def total(own, recv, base):
        acc = own[base].astype(F32)
        for k in range(1, 8):
            acc += recv[k].astype(F32)
        return acc

    t3_own[...] = total(t1_own, t1_recv, z).astype(BF16)
    t4_own[...] = total(t2_own, t2_recv, y).astype(BF16)
    c3 = []
    for k in (4, 3, 5, 2, 6, 1, 7):
        c3.append(push(t3_own.at[turn(y, k)], t3_recv.at[k], t3_s.at[k], t3_r.at[k], at_y(k)))
        c3.append(push(t4_own.at[turn(z, k)], t4_recv.at[k], t4_s.at[k], t4_r.at[k], at_z(k)))

    for copy in c2:
        copy.wait_recv()
    a_cell = total(a2_own, a2_recv, y)
    b_cell = total(b2_own, b2_recv, z)
    quarter = iota((8, 128), 1) // 32
    for xh, source_cell in ((0, a_cell), (1, b_cell)):
        for xl in range(4):
            acc = jnp.zeros((8, 128), F32)
            for g in range(4):
                piece = source_cell[8 * g:8 * g + 8]
                if g != xl:
                    piece = pltpu.roll(piece, 32 * ((g - xl) % 4), 1)
                acc = jnp.where(quarter == g, piece, acc)
            both = jnp.concatenate([acc, a_cell[32 + 8 * xh:40 + 8 * xh]], axis=0)
            x_own[xh * 4 + xl] = both.astype(BF16)
    cx = []
    for k in (4, 3, 5, 2, 6, 1, 7):
        cx.append(push(x_own.at[turn(x, k)], x_recv.at[k], x_s.at[k], x_r.at[k], at_x(k)))

    for copy in c3:
        copy.wait_recv()
    left = total(t3_own, t3_recv, y)
    right = total(t4_own, t4_recv, z)
    touched_ref[:, 0:128] = left[0:8]
    touched_ref[:, 128:256] = left[8:16]
    touched_ref[:, 256:384] = right[0:8]
    touched_ref[:, 384:512] = right[8:16]

    for copy in cx:
        copy.wait_recv()
    scale = 1.0 / math.sqrt(TOK * 16 * 64)
    last = total(x_own, x_recv, x) * scale
    turned = jnp.transpose(jnp.concatenate([last, jnp.zeros((112, 128), F32)], axis=0))
    flip[...] = turned
    for g in range(4):
        gin_ref[:, 8 * g:8 * g + 8] = turned[32 * g:32 * g + 32, 0:8]
    gout_ref[...] = flip[pl.ds(pl.multiple_of(lax.rem(x, 4) * 32, 32), 32), :][:, 8:16]

    for copy in sent:
        copy.wait_send()


def on_device(tokens, cotangent, hist_len, item_owner, item_slot, w_in, w_out):
    vmem = pl.BlockSpec(memory_space=pltpu.VMEM)
    hbm = pl.BlockSpec(memory_space=pl.ANY)

    def buf(*shape, dtype=BF16):
        return pltpu.VMEM(shape, dtype)

    def sems(n):
        return pltpu.SemaphoreType.DMA((n,))

    return pl.pallas_call(
        kernel,
        out_shape=(
            jax.ShapeDtypeStruct((8, 512), F32),
            jax.ShapeDtypeStruct((32, 32), F32),
            jax.ShapeDtypeStruct((32, 8), F32),
        ),
        in_specs=[pl.BlockSpec(memory_space=pltpu.SMEM), vmem, vmem, vmem, vmem, hbm, hbm],
        out_specs=(vmem, vmem, vmem),
        scratch_shapes=[
            buf(512, 2048), buf(512, 512), buf(TOK, 2048, dtype=F32), buf(TOK, 2048),
            buf(256, 2048), buf(256, 256), buf(256, 256), buf(256, 512),
            buf(2, TOK, 256), buf(2, TOK, 256),
            buf(16, 16, 640), buf(16, 16, 640),
            buf(8, 8, 48, 128), buf(7, 8, 48, 128), buf(8, 8, 32, 128), buf(7, 8, 32, 128),
            buf(8, 8, 16, 128), buf(8, 8, 16, 128), buf(8, 8, 16, 128), buf(8, 8, 16, 128),
            buf(8, 48, 128), buf(8, 48, 128), buf(8, 32, 128), buf(8, 32, 128),
            buf(8, 16, 128), buf(8, 16, 128), buf(8, 16, 128), buf(8, 16, 128),
            buf(8, 16, 128), buf(8, 16, 128), buf(128, 128, dtype=F32),
            sems(5), sems(7), sems(7), sems(16), sems(16),
            sems(7), sems(7), sems(7), sems(7),
        ] + [sems(8)] * 14,
        compiler_params=pltpu.CompilerParams(
            collective_id=0, has_side_effects=True, vmem_limit_bytes=40 * 1024 * 1024
        ),
    )(
        hist_len, tokens, cotangent, item_owner.reshape(1, TOK), item_slot.reshape(1, TOK),
        w_in, w_out,
    )


def solution(mesh):
    return jax.shard_map(
        on_device,
        mesh=mesh,
        in_specs=(
            P(("table", "rep"), None),
            P(("table", "rep"), None),
            P(("table", "rep")),
            P(("table", "rep"), None),
            P(("table", "rep")),
            P(),
            P(),
        ),
        out_specs=(P(("table", "rep"), None), P("table", "rep"), P("table", "rep")),
        check_vma=False,
    )
```

```python
import math

import jax
import jax.numpy as jnp
from jax import lax
from jax.experimental import pallas as pl
from jax.experimental.pallas import tpu as pltpu
from jax.sharding import PartitionSpec as P

D = 512
HEADS = 4
DH = 128
SLOTS_H = 64
TOK = 128
F32 = jnp.float32
BF16 = jnp.bfloat16
MESH = pl.DeviceIdType.MESH
NT = (((1,), (1,)), ((), ()))
TN = (((0,), (0,)), ((), ()))


def mm(a, b, dims=(((1,), (0,)), ((), ()))):
    return lax.dot_general(a, b, dims, preferred_element_type=F32)


def norm_rows(values):
    middle = jnp.mean(values, axis=-1, keepdims=True)
    centered = values - middle
    inverse = lax.rsqrt(jnp.mean(centered * centered, axis=-1, keepdims=True) + 1e-06)
    return centered * inverse, inverse


def norm_back(upstream, normed, inverse):
    first = jnp.mean(upstream, axis=-1, keepdims=True)
    second = jnp.mean(upstream * normed, axis=-1, keepdims=True)
    return inverse * (upstream - first - normed * second)


def sigmoid(values):
    return 0.5 * jnp.tanh(0.5 * values) + 0.5


def iota(shape, dim):
    return lax.broadcasted_iota(jnp.int32, shape, dim)


def cells(block):
    lo = block[:, :128].reshape(64, 8, 128)
    hi = block[:, 128:].reshape(64, 8, 128)
    return jnp.concatenate([lo, hi], axis=1).reshape(8, 8, 16, 128).astype(BF16)


def kernel(
    len_hbm, tok_hbm, cot_hbm, own_hbm, slot_hbm, w_in_hbm, w_out_hbm,
    touched_ref, last_ref,
    len_ref, tok_ref, cot_ref, own_ref, slot_ref, w_in, w_out, sgrad, hid, d2, nb2, gt2, er2, nbf, gtf,
    out_rows, in_rows, a_own, a_recv, b_own, b_recv,
    t1_own, t1_recv, t2_own, t2_recv,
    a2_own, a2_recv, b2_own, b2_recv, t3_own, t3_recv, t4_own, t4_recv,
    x_own, x_recv, o1_own, o1_recv, o2_own, o2_recv, o3_own, o3_recv, flip,
    w_sem, pair_s, pair_r, row_s, row_r, a_s, a_r, b_s, b_r,
    t1_s, t1_r, t2_s, t2_r, a2_s, a2_r, b2_s, b2_r, t3_s, t3_r, t4_s, t4_r, x_s, x_r,
    o1_s, o1_r, o2_s, o2_r, o3_s, o3_r,
):
    t = lax.axis_index("table")
    r = lax.axis_index("rep")
    x, core = lax.div(t, 2), lax.rem(t, 2)
    z, y = lax.div(r, 8), lax.rem(r, 8)

    def turn(base, k, n=8):
        return lax.rem(base + (k + n), n)

    def at_z(k):
        return (t, turn(z, k) * 8 + y)

    def at_y(k):
        return (t, z * 8 + turn(y, k))

    def at_t(k):
        return (turn(t, k, 16), r)

    def at_x(k):
        return (turn(x, k) * 2 + core, r)

    mate = (x * 2 + (1 - core), r)
    sent = []

    def push(src, dst, ssem, rsem, where):
        copy = pltpu.make_async_remote_copy(
            src_ref=src, dst_ref=dst, send_sem=ssem, recv_sem=rsem,
            device_id=where, device_id_type=MESH,
        )
        copy.start()
        sent.append(copy)
        return copy

    barrier = pltpu.get_barrier_semaphore()
    partners = [at_z(k) for k in range(1, 8)] + [at_y(k) for k in range(1, 8)]
    partners += [at_t(k) for k in range(1, 16)]
    for where in partners:
        pl.semaphore_signal(barrier, inc=1, device_id=where, device_id_type=MESH)

    small = []
    for n, (there, here) in enumerate((
        (tok_hbm, tok_ref), (len_hbm, len_ref), (cot_hbm, cot_ref), (own_hbm, own_ref), (slot_hbm, slot_ref),
    )):
        small.append(pltpu.make_async_copy(there, here, w_sem.at[5 + n]))
        small[-1].start()
    loads = []
    for b in range(4):
        cols = pl.ds(b * 512, 512)
        loads.append(pltpu.make_async_copy(w_in_hbm.at[:, cols], w_in.at[:, cols], w_sem.at[b]))
    loads.append(pltpu.make_async_copy(w_out_hbm, w_out, w_sem.at[4]))
    for load in loads:
        load.start()

    small[1].wait()
    len0, len1 = len_ref[0], len_ref[1]
    ri, ci = iota((TOK, TOK), 0), iota((TOK, TOK), 1)
    same = (ri < SLOTS_H) == (ci < SLOTS_H)
    limit = jnp.where(ci < SLOTS_H, len0, len1 + SLOTS_H)
    keep = same & (ci <= ri) & (ci < limit)
    rows_i = iota((TOK, D), 0)
    valid = rows_i < jnp.where(rows_i < SLOTS_H, len0, len1 + SLOTS_H)

    small[0].wait()
    normed, inv_tok = norm_rows(tok_ref[...].astype(F32))
    nb = normed.astype(BF16)
    pi, pj = iota((D, D), 0), iota((D, D), 1)
    source = ((pj // 32) % 8) * 64 + (pj // 256) * 32 + pj % 32
    perm = jnp.where(pi == source, 1.0, 0.0).astype(BF16)
    nbp = mm(nb, perm).astype(BF16)
    nbf[0] = nbp[:, :256]
    nbf[1] = nbp[:, 256:]
    nb2[0:TOK, :] = nbf[core]
    small[2].wait()
    err = jnp.where(valid, cot_ref[...], jnp.zeros((TOK, D), BF16))
    er2[0:TOK, :] = err
    for b in range(4):
        cols = pl.ds(b * 512, 512)
        loads[b].wait()
        pre = mm(nb, w_in[:, cols])
        sig = sigmoid(pre)
        hid[:, cols] = (pre * sig).astype(BF16)
        sgrad[:, cols] = sig * (1.0 + pre * (1.0 - sig))
    pl.semaphore_wait(barrier, len(partners))
    pair = [
        push(er2.at[pl.ds(0, TOK)], er2.at[pl.ds(TOK, TOK)], pair_s.at[0], pair_r.at[0], mate),
        push(nbf.at[1 - core], nb2.at[pl.ds(TOK, TOK)], pair_s.at[1], pair_r.at[1], mate),
    ]
    score_scale = 1.0 / math.sqrt(DH)
    atts, slopes, mixes = [], [], []
    for h in range(HEADS):
        query = hid[:, 1024 + h * DH:1024 + (h + 1) * DH]
        keys = hid[:, 1536 + h * DH:1536 + (h + 1) * DH]
        vals = hid[:, 512 + h * DH:512 + (h + 1) * DH]
        score = mm(query, keys, NT) * score_scale
        sig = sigmoid(score)
        att = jnp.where(keep, score * sig * (1.0 / SLOTS_H), 0.0).astype(BF16)
        slopes.append(jnp.where(keep, sig * (1.0 + score * (1.0 - sig)) * (1.0 / SLOTS_H), 0.0))
        atts.append(att)
        mixes.append(mm(att, vals))
    on_mix, inv_mix = norm_rows(jnp.concatenate(mixes, axis=1))
    gate = hid[:, 0:512].astype(F32)
    gated = (on_mix * gate).astype(BF16)
    gtp = mm(gated, perm).astype(BF16)
    gtf[0] = gtp[:, :256]
    gtf[1] = gtp[:, 256:]
    gt2[0:TOK, :] = gtf[core]
    pair.append(push(gtf.at[1 - core], gt2.at[pl.ds(TOK, TOK)], pair_s.at[2], pair_r.at[2], mate))

    loads[4].wait()
    dgate = mm(err, w_out[...], NT)

    def give(b, value):
        cols = pl.ds(b * 512, 512)
        d2[0:TOK, cols] = (value * sgrad[:, cols]).astype(BF16)
        pair.append(push(
            d2.at[pl.ds(0, TOK), cols], d2.at[pl.ds(TOK, TOK), cols],
            pair_s.at[3 + b], pair_r.at[3 + b], mate,
        ))

    give(0, dgate * on_mix)
    dmix = norm_back(dgate * gate, on_mix, inv_mix).astype(BF16)
    gv, gq, gk = [], [], []
    for h in range(HEADS):
        query = hid[:, 1024 + h * DH:1024 + (h + 1) * DH]
        keys = hid[:, 1536 + h * DH:1536 + (h + 1) * DH]
        vals = hid[:, 512 + h * DH:512 + (h + 1) * DH]
        part = dmix[:, h * DH:(h + 1) * DH]
        dscore = (mm(part, vals, NT) * slopes[h]).astype(BF16)
        gv.append(mm(atts[h], part, TN))
        gq.append(mm(dscore, keys) * score_scale)
        gk.append(mm(dscore, query, TN) * score_scale)
    give(1, jnp.concatenate(gv, axis=1))
    give(2, jnp.concatenate(gq, axis=1))
    give(3, jnp.concatenate(gk, axis=1))
    dnorm = mm(d2[0:TOK, 0:512], w_in[:, 0:512], NT)
    for b in range(1, 4):
        dnorm += mm(d2[0:TOK, b * 512:(b + 1) * 512], w_in[:, b * 512:(b + 1) * 512], NT)
    rows = (err.astype(F32) + norm_back(dnorm, normed, inv_tok)).astype(BF16)

    small[3].wait()
    small[4].wait()
    owner = own_ref[...]
    slot = slot_ref[...]
    mine = iota((16, TOK), 0) == owner
    hot = jnp.where(mine, 1.0, 0.0)
    before = jnp.where(ri < ci, 1.0, 0.0).astype(BF16)
    earlier = mm(hot.astype(BF16), before)
    placed = jnp.sum(earlier * hot, axis=0, keepdims=True)
    key = owner.astype(F32) * 16.0 + placed
    pick = jnp.where(iota((256, TOK), 0).astype(F32) == key, 1.0, 0.0)
    packed = mm(pick.astype(BF16), rows).astype(BF16)
    s_z = jnp.sum(pick * (slot // 64).astype(F32), axis=1, keepdims=True)
    s_y = jnp.sum(pick * ((slot // 8) % 8).astype(F32), axis=1, keepdims=True)
    s_i = jnp.sum(pick * (slot % 8).astype(F32), axis=1, keepdims=True)
    lane = iota((256, 128), 1)
    tail = jnp.where(lane == 0, s_z, jnp.where(lane == 1, s_y, jnp.where(lane == 2, s_i, 0.0)))
    out_rows[:, :, 0:512] = packed.reshape(16, 16, 512)
    out_rows[:, :, 512:640] = tail.astype(BF16).reshape(16, 16, 128)
    in_rows[0] = out_rows[t]
    row_copies = []
    for k in (8, 7, 9, 6, 10, 5, 11, 4, 12, 3, 13, 2, 14, 1, 15):
        row_copies.append(push(
            out_rows.at[turn(t, k, 16)], in_rows.at[k], row_s.at[k], row_r.at[k], at_t(k)
        ))

    for copy in pair[:3]:
        copy.wait_recv()
    o1_own[...] = mm(gt2[...], er2[...], TN).astype(BF16).reshape(8, 32, 512)
    far = (4, 3, 5, 2, 6, 1, 7)
    co1 = [push(o1_own.at[turn(x, k)], o1_recv.at[k], o1_s.at[k], o1_r.at[k], at_x(k)) for k in far]
    for copy in pair[3:]:
        copy.wait_recv()

    def block(k):
        d = turn(z, k)
        cols = pl.ds(pl.multiple_of(d * 256, 256), 256)
        part = mm(d2[:, cols], nb2[...], TN)
        a_own[d] = part[:, :128].reshape(8, 32, 128).astype(BF16)
        b_own[:, d] = part[:, 128:].reshape(8, 32, 128).astype(BF16)

    def spread(own, recv, ssem, rsem, base, where, k):
        return push(own.at[turn(base, k)], recv.at[k], ssem.at[k], rsem.at[k], where(k))

    ca, cb = [], []
    for k in far:
        block(k)
        ca.append(spread(a_own, a_recv, a_s, a_r, z, at_z, k))
    block(0)
    for k in far:
        cb.append(spread(b_own, b_recv, b_s, b_r, y, at_y, k))

    def total(own, recv, base):
        acc = own[base].astype(F32)
        for k in range(1, 8):
            acc += recv[k].astype(F32)
        return acc

    for copy in row_copies:
        copy.wait_recv()
    arrived = in_rows[...].reshape(256, 640)
    numbers = arrived[:, 512:640].astype(F32)
    by_z = jnp.where(lane == 0, 64.0, jnp.where(lane == 1, 8.0, jnp.where(lane == 2, 1.0, 0.0)))
    by_y = jnp.where(lane == 0, 8.0, jnp.where(lane == 1, 64.0, jnp.where(lane == 2, 1.0, 0.0)))
    line = iota((256, 512), 1).astype(F32)
    hot_z = jnp.where(line == jnp.sum(numbers * by_z, axis=1, keepdims=True), 1.0, 0.0)
    hot_y = jnp.where(line == jnp.sum(numbers * by_y, axis=1, keepdims=True), 1.0, 0.0)
    t1_own[...] = cells(mm(hot_z.astype(BF16), arrived[:, 0:256], TN))
    t2_own[...] = cells(mm(hot_y.astype(BF16), arrived[:, 256:512], TN))
    ct = []
    for k in (4, 3, 5, 2, 6, 1, 7):
        ct.append(push(t1_own.at[turn(z, k)], t1_recv.at[k], t1_s.at[k], t1_r.at[k], at_z(k)))
        ct.append(push(t2_own.at[turn(y, k)], t2_recv.at[k], t2_s.at[k], t2_r.at[k], at_y(k)))

    for copy in co1:
        copy.wait_recv()
    tall = jnp.transpose(total(o1_own, o1_recv, x)).reshape(8, 4, 16, 32)
    o2_own[...] = jnp.concatenate([tall[:, g] for g in range(4)], axis=-1).astype(BF16)
    co2 = [push(o2_own.at[turn(z, k)], o2_recv.at[k], o2_s.at[k], o2_r.at[k], at_z(k)) for k in far]

    for copy in ca:
        copy.wait_recv()
    a2_own[...] = total(a_own, a_recv, z).astype(BF16)
    c2 = []
    for k in (4, 3, 5, 2, 6, 1, 7):
        c2.append(push(a2_own.at[turn(y, k)], a2_recv.at[k], a2_s.at[k], a2_r.at[k], at_y(k)))
    for copy in cb:
        copy.wait_recv()
    b2_own[...] = total(b_own, b_recv, y).astype(BF16)
    for k in (4, 3, 5, 2, 6, 1, 7):
        c2.append(push(b2_own.at[turn(z, k)], b2_recv.at[k], b2_s.at[k], b2_r.at[k], at_z(k)))

    for copy in ct:
        copy.wait_recv()

    t3_own[...] = total(t1_own, t1_recv, z).astype(BF16)
    t4_own[...] = total(t2_own, t2_recv, y).astype(BF16)
    c3 = []
    for k in (4, 3, 5, 2, 6, 1, 7):
        c3.append(push(t3_own.at[turn(y, k)], t3_recv.at[k], t3_s.at[k], t3_r.at[k], at_y(k)))
        c3.append(push(t4_own.at[turn(z, k)], t4_recv.at[k], t4_s.at[k], t4_r.at[k], at_z(k)))

    for copy in co2:
        copy.wait_recv()
    o3_own[...] = total(o2_own, o2_recv, z).astype(BF16)
    co3 = [push(o3_own, o3_recv.at[k], o3_s.at[k], o3_r.at[k], at_y(k)) for k in far]

    for copy in c2:
        copy.wait_recv()
    a_cell = total(a2_own, a2_recv, y)
    b_cell = total(b2_own, b2_recv, z)
    quarter = iota((8, 128), 1) // 32
    for xh, source_cell in ((0, a_cell), (1, b_cell)):
        for xl in range(4):
            acc = jnp.zeros((8, 128), F32)
            for g in range(4):
                piece = source_cell[8 * g:8 * g + 8]
                if g != xl:
                    piece = pltpu.roll(piece, 32 * ((g - xl) % 4), 1)
                acc = jnp.where(quarter == g, piece, acc)
            x_own[xh * 4 + xl] = acc
    cx = []
    for k in (4, 3, 5, 2, 6, 1, 7):
        cx.append(push(x_own.at[turn(x, k)], x_recv.at[k], x_s.at[k], x_r.at[k], at_x(k)))

    for copy in c3:
        copy.wait_recv()
    left = total(t3_own, t3_recv, y)
    right = total(t4_own, t4_recv, z)
    touched_ref[:, 0:128] = left[0:8]
    touched_ref[:, 128:256] = left[8:16]
    touched_ref[:, 256:384] = right[0:8]
    touched_ref[:, 384:512] = right[8:16]

    for copy in co3:
        copy.wait_recv()
    flip[...] = o3_own[...].astype(F32)
    for k in range(1, 8):
        flip[...] += o3_recv[k].astype(F32)
    part = flip[pl.ds(pl.multiple_of(lax.rem(y, 2) * 8, 8), 8), :]
    acc = part
    for g in range(1, 4):
        acc = jnp.where(lax.div(y, 2) == g, pltpu.roll(part, 128 - 32 * g, 1), acc)
    last_ref[8:16, :] = acc
    for copy in cx:
        copy.wait_recv()
    last_ref[0:8, :] = total(x_own, x_recv, x)

    for copy in sent:
        copy.wait_send()


def finish(rows_ref, last_ref, touched_ref, gin_ref, gout_ref):
    touched_ref[...] = rows_ref[...]
    scale = 1.0 / math.sqrt(TOK * 16 * 64)
    tall = jnp.concatenate([last_ref[...] * scale, jnp.zeros((112, 128), F32)], axis=0)
    turned = jnp.transpose(tall)
    for g in range(4):
        gin_ref[:, 8 * g:8 * g + 8] = turned[32 * g:32 * g + 32, 0:8]
    gout_ref[...] = last_ref[8:16, 0:32] * scale


def on_device(tokens, cotangent, hist_len, item_owner, item_slot, w_in, w_out):
    vmem = pl.BlockSpec(memory_space=pltpu.VMEM)
    hbm = pl.BlockSpec(memory_space=pltpu.HBM)

    def buf(*shape, dtype=BF16):
        return pltpu.VMEM(shape, dtype)

    def sems(n):
        return pltpu.SemaphoreType.DMA((n,))

    rows, last = pl.pallas_call(
        kernel,
        out_shape=(
            jax.ShapeDtypeStruct((8, 512), F32),
            jax.ShapeDtypeStruct((16, 128), F32),
        ),
        in_specs=[hbm] * 7,
        out_specs=(vmem, vmem),
        scratch_shapes=[
            pltpu.SMEM((2,), jnp.int32), buf(TOK, D), buf(TOK, D),
            buf(1, TOK, dtype=jnp.int32), buf(1, TOK, dtype=jnp.int32),
            buf(512, 2048), buf(512, 512), buf(TOK, 2048, dtype=F32), buf(TOK, 2048),
            buf(256, 2048), buf(256, 256), buf(256, 256), buf(256, 512),
            buf(2, TOK, 256), buf(2, TOK, 256),
            buf(16, 16, 640), buf(16, 16, 640),
            buf(8, 8, 32, 128), buf(8, 8, 32, 128), buf(8, 8, 32, 128), buf(8, 8, 32, 128),
            buf(8, 8, 16, 128), buf(8, 8, 16, 128), buf(8, 8, 16, 128), buf(8, 8, 16, 128),
            buf(8, 32, 128), buf(8, 32, 128), buf(8, 32, 128), buf(8, 32, 128),
            buf(8, 16, 128), buf(8, 16, 128), buf(8, 16, 128), buf(8, 16, 128),
            buf(8, 8, 128, dtype=F32), buf(8, 8, 128, dtype=F32),
            buf(8, 32, 512), buf(8, 32, 512), buf(8, 16, 128), buf(8, 16, 128),
            buf(16, 128), buf(8, 16, 128), buf(16, 128, dtype=F32),
            sems(10), sems(7), sems(7), sems(16), sems(16),
        ] + [sems(8)] * 24,
        compiler_params=pltpu.CompilerParams(
            collective_id=0, has_side_effects=True, vmem_limit_bytes=62 * 1024 * 1024
        ),
    )(
        hist_len, tokens, cotangent, item_owner.reshape(1, TOK), item_slot.reshape(1, TOK),
        w_in, w_out,
    )
    touched, grad_in, grad_out = pl.pallas_call(
        finish,
        out_shape=(
            jax.ShapeDtypeStruct((8, 512), F32),
            jax.ShapeDtypeStruct((32, 32), F32),
            jax.ShapeDtypeStruct((8, 32), F32),
        ),
        in_specs=[vmem, vmem],
        out_specs=(vmem, vmem, vmem),
        compiler_params=pltpu.CompilerParams(vmem_limit_bytes=62 * 1024 * 1024),
    )(rows, last)
    return touched, grad_in, grad_out.T


def solution(mesh):
    return jax.shard_map(
        on_device,
        mesh=mesh,
        in_specs=(
            P(("table", "rep"), None),
            P(("table", "rep"), None),
            P(("table", "rep")),
            P(("table", "rep"), None),
            P(("table", "rep")),
            P(),
            P(),
        ),
        out_specs=(P(("table", "rep"), None), P("table", "rep"), P("table", "rep")),
        check_vma=False,
    )
```

```python
import math

import jax
import jax.numpy as jnp
from jax import lax
from jax.experimental import pallas as pl
from jax.experimental.pallas import tpu as pltpu
from jax.sharding import PartitionSpec as P

D = 512
HEADS = 4
DH = 128
SLOTS_H = 64
TOK = 128
F32 = jnp.float32
BF16 = jnp.bfloat16
MESH = pl.DeviceIdType.MESH
NT = (((1,), (1,)), ((), ()))
TN = (((0,), (0,)), ((), ()))


def mm(a, b, dims=(((1,), (0,)), ((), ()))):
    return lax.dot_general(a, b, dims, preferred_element_type=F32)


def norm_rows(values):
    middle = jnp.mean(values, axis=-1, keepdims=True)
    centered = values - middle
    inverse = lax.rsqrt(jnp.mean(centered * centered, axis=-1, keepdims=True) + 1e-06)
    return centered * inverse, inverse


def norm_back(upstream, normed, inverse):
    first = jnp.mean(upstream, axis=-1, keepdims=True)
    second = jnp.mean(upstream * normed, axis=-1, keepdims=True)
    return inverse * (upstream - first - normed * second)


def sigmoid(values):
    return 0.5 * jnp.tanh(0.5 * values) + 0.5


def iota(shape, dim):
    return lax.broadcasted_iota(jnp.int32, shape, dim)


def cells(block):
    lo = block[:, :128].reshape(64, 8, 128)
    hi = block[:, 128:].reshape(64, 8, 128)
    return jnp.concatenate([lo, hi], axis=1).reshape(8, 8, 16, 128).astype(BF16)


def kernel(
    len_hbm, tok_hbm, cot_hbm, own_hbm, slot_hbm, w_in_hbm, w_out_hbm,
    touched_ref, last_ref,
    len_ref, tok_ref, cot_ref, own_ref, slot_ref, w_in, w_out, sgrad, hid, d2, nb2, gt2, er2, nbf, gtf,
    out_rows, in_rows, out_nums, in_nums, a_own, a_recv, a_late, b_own, b_recv, b_late,
    t1_own, t1_recv, t2_own, t2_recv,
    a2_own, a2_recv, b2_own, b2_recv, t3_own, t3_recv, t4_own, t4_recv,
    x_own, x_recv, o1_own, o1_recv, o2_own, o2_recv, o3_own, o3_recv, flip,
    w_sem, pair_s, pair_r, row_s, row_r, a_s, a_r, b_s, b_r,
    t1_s, t1_r, t2_s, t2_r, a2_s, a2_r, b2_s, b2_r, t3_s, t3_r, t4_s, t4_r, x_s, x_r,
    o1_s, o1_r, o2_s, o2_r, o3_s, o3_r, al_s, al_r, bl_s, bl_r, num_s, num_r,
):
    t = lax.axis_index("table")
    r = lax.axis_index("rep")
    x, core = lax.div(t, 2), lax.rem(t, 2)
    z, y = lax.div(r, 8), lax.rem(r, 8)

    def turn(base, k, n=8):
        return lax.rem(base + (k + n), n)

    def at_z(k):
        return (t, turn(z, k) * 8 + y)

    def at_y(k):
        return (t, z * 8 + turn(y, k))

    def at_t(k):
        return (turn(t, k, 16), r)

    def at_x(k):
        return (turn(x, k) * 2 + core, r)

    mate = (x * 2 + (1 - core), r)
    sent = []

    def push(src, dst, ssem, rsem, where):
        pltpu.make_async_remote_copy(
            src_ref=src, dst_ref=dst, send_sem=ssem, recv_sem=rsem,
            device_id=where, device_id_type=MESH,
        ).start()

    def settle(ref, sem):
        pltpu.make_async_copy(ref, ref, sem).wait()

    far = (4, 3, 5, 2, 6, 1, 7)

    def spread(own, recv, ssem, rsem, base, where):
        for k in far:
            push(own.at[turn(base, k)], recv.at[k], ssem, rsem, where(k))
        sent.append((own.at[pl.ds(0, 7)], ssem))

    small = []
    for n, (there, here) in enumerate((
        (tok_hbm, tok_ref), (len_hbm, len_ref), (cot_hbm, cot_ref), (own_hbm, own_ref), (slot_hbm, slot_ref),
    )):
        small.append(pltpu.make_async_copy(there, here, w_sem.at[5 + n]))
        small[-1].start()
    loads = []
    for b in range(4):
        cols = pl.ds(b * 512, 512)
        loads.append(pltpu.make_async_copy(w_in_hbm.at[:, cols], w_in.at[:, cols], w_sem.at[b]))
    loads.append(pltpu.make_async_copy(w_out_hbm, w_out, w_sem.at[4]))
    for load in loads:
        load.start()

    barrier = pltpu.get_barrier_semaphore()
    partners = [at_z(k) for k in range(1, 8)] + [at_y(k) for k in range(1, 8)]
    partners += [at_t(k) for k in range(1, 16)]
    for where in partners:
        pl.semaphore_signal(barrier, inc=1, device_id=where, device_id_type=MESH)

    small[1].wait()
    len0, len1 = len_ref[0], len_ref[1]
    ri, ci = iota((TOK, TOK), 0), iota((TOK, TOK), 1)
    same = (ri < SLOTS_H) == (ci < SLOTS_H)
    limit = jnp.where(ci < SLOTS_H, len0, len1 + SLOTS_H)
    keep = same & (ci <= ri) & (ci < limit)
    rows_i = iota((TOK, D), 0)
    valid = rows_i < jnp.where(rows_i < SLOTS_H, len0, len1 + SLOTS_H)

    small[0].wait()
    normed, inv_tok = norm_rows(tok_ref[...].astype(F32))
    nb = normed.astype(BF16)
    pi, pj = iota((D, D), 0), iota((D, D), 1)
    source = ((pj // 32) % 8) * 64 + (pj // 256) * 32 + pj % 32
    perm = jnp.where(pi == source, 1.0, 0.0).astype(BF16)
    nbp = mm(nb, perm).astype(BF16)
    nbf[0] = nbp[:, :256]
    nbf[1] = nbp[:, 256:]
    nb2[0:TOK, :] = nbf[core]
    small[2].wait()
    err = jnp.where(valid, cot_ref[...], jnp.zeros((TOK, D), BF16))
    er2[0:TOK, :] = err
    for b in range(4):
        cols = pl.ds(b * 512, 512)
        loads[b].wait()
        pre = mm(nb, w_in[:, cols])
        sig = sigmoid(pre)
        hid[:, cols] = (pre * sig).astype(BF16)
        sgrad[:, cols] = sig * (1.0 + pre * (1.0 - sig))
    pl.semaphore_wait(barrier, len(partners))
    own_half, mate_half = pl.ds(0, TOK), pl.ds(TOK, TOK)
    push(er2.at[own_half], er2.at[mate_half], pair_s.at[0], pair_r.at[0], mate)
    push(nbf.at[1 - core], nb2.at[mate_half], pair_s.at[1], pair_r.at[1], mate)
    score_scale = 1.0 / math.sqrt(DH)
    atts, slopes, mixes = [], [], []
    for h in range(HEADS):
        query = hid[:, 1024 + h * DH:1024 + (h + 1) * DH]
        keys = hid[:, 1536 + h * DH:1536 + (h + 1) * DH]
        vals = hid[:, 512 + h * DH:512 + (h + 1) * DH]
        score = mm(query, keys, NT) * score_scale
        sig = sigmoid(score)
        att = jnp.where(keep, score * sig * (1.0 / SLOTS_H), 0.0).astype(BF16)
        slopes.append(jnp.where(keep, sig * (1.0 + score * (1.0 - sig)) * (1.0 / SLOTS_H), 0.0))
        atts.append(att)
        mixes.append(mm(att, vals))
    on_mix, inv_mix = norm_rows(jnp.concatenate(mixes, axis=1))
    gate = hid[:, 0:512].astype(F32)
    gated = (on_mix * gate).astype(BF16)
    gtp = mm(gated, perm).astype(BF16)
    gtf[0] = gtp[:, :256]
    gtf[1] = gtp[:, 256:]
    gt2[0:TOK, :] = gtf[core]
    push(gtf.at[1 - core], gt2.at[mate_half], pair_s.at[2], pair_r.at[2], mate)

    loads[4].wait()
    dgate = mm(err, w_out[...], NT)

    def give(b, value):
        cols = pl.ds(b * 512, 512)
        d2[0:TOK, cols] = (value * sgrad[:, cols]).astype(BF16)
        push(d2.at[own_half, cols], d2.at[mate_half, cols], pair_s.at[3], pair_r.at[3], mate)

    give(0, dgate * on_mix)
    dmix = norm_back(dgate * gate, on_mix, inv_mix).astype(BF16)
    gv, gq, gk = [], [], []
    for h in range(HEADS):
        query = hid[:, 1024 + h * DH:1024 + (h + 1) * DH]
        keys = hid[:, 1536 + h * DH:1536 + (h + 1) * DH]
        vals = hid[:, 512 + h * DH:512 + (h + 1) * DH]
        part = dmix[:, h * DH:(h + 1) * DH]
        dscore = (mm(part, vals, NT) * slopes[h]).astype(BF16)
        gv.append(mm(atts[h], part, TN))
        gq.append(mm(dscore, keys) * score_scale)
        gk.append(mm(dscore, query, TN) * score_scale)
    give(1, jnp.concatenate(gv, axis=1))
    give(2, jnp.concatenate(gq, axis=1))
    give(3, jnp.concatenate(gk, axis=1))
    dnorm = mm(d2[0:TOK, 0:512], w_in[:, 0:512], NT)
    for b in range(1, 4):
        dnorm += mm(d2[0:TOK, b * 512:(b + 1) * 512], w_in[:, b * 512:(b + 1) * 512], NT)
    rows = (err.astype(F32) + norm_back(dnorm, normed, inv_tok)).astype(BF16)

    small[3].wait()
    small[4].wait()
    owner = own_ref[...]
    slot = slot_ref[...]
    ahead = lax.rem(owner - t + 16, 16)
    hot = jnp.where(iota((16, TOK), 0) == ahead, 1.0, 0.0)
    before = jnp.where(ri < ci, 1.0, 0.0).astype(BF16)
    earlier = mm(hot.astype(BF16), before)
    placed = jnp.sum(earlier * hot, axis=0, keepdims=True)
    key = ahead.astype(F32) * 16.0 + placed
    pick = jnp.where(iota((256, TOK), 0).astype(F32) == key, 1.0, 0.0)
    out_rows[...] = mm(pick.astype(BF16), rows).astype(BF16).reshape(16, 16, 512)
    line = lax.rem(ahead, 8).astype(F32) * 16.0 + placed
    spot = jnp.where(ri.astype(F32) == line, 1.0, 0.0).astype(BF16)
    high = mm((hot * (slot // 16).astype(F32)).astype(BF16), spot, NT)
    low = mm((hot * (slot % 16).astype(F32)).astype(BF16), spot, NT)
    numbers = high * 16.0 + low
    for k in range(16):
        out_nums[k] = numbers[k:k + 1, :]
    for k in (8, 7, 9, 6, 10, 5, 11, 4, 12, 3, 13, 2, 14, 1, 15):
        push(out_nums.at[k], in_nums.at[k], num_s, num_r, at_t(k))
        push(out_rows.at[k], in_rows.at[k], row_s, row_r, at_t(k))
    in_rows[0] = out_rows[0]
    in_nums[0] = out_nums[0]

    settle(er2.at[mate_half], pair_r.at[0])
    settle(nb2.at[mate_half], pair_r.at[1])
    settle(gt2.at[mate_half], pair_r.at[2])
    o1_own[...] = mm(gt2[...], er2[...], TN).astype(BF16).reshape(8, 32, 512)
    spread(o1_own, o1_recv, o1_s, o1_r, x, at_x)
    settle(d2.at[mate_half], pair_r.at[3])

    def block(k):
        d = turn(z, k)
        cols = pl.ds(pl.multiple_of(d * 256, 256), 256)
        part = mm(d2[:, cols], nb2[...], TN)
        a_own[d] = part[:, :128].reshape(8, 32, 128).astype(BF16)
        b_own[:, d] = part[:, 128:].reshape(8, 32, 128).astype(BF16)

    for k in (4, 3, -3, 2, -2, 1, -1, 0):
        block(k)

    def sides(base):
        side = 1 - 2 * lax.rem(base, 2)
        return ((pl.ds(0, 4), side), (pl.ds(4, 4), -side))

    def swap(own, recv, ssem, rsem, base, where):
        for j in (3, 2, 1, 0):
            for part, side in sides(base):
                push(
                    own.at[turn(base, side * (j + 1)), part], recv.at[j, part],
                    ssem, rsem, where(side),
                )
        sent.append((own.at[pl.ds(0, 4)], ssem))

    def send_on(own, recv, got, late, ssem, rsem, base, where):
        settle(recv, got)
        for j in (3, 2, 1, 0):
            for part, side in sides(base):
                d = turn(base, -side * j)
                own[d, part] = (own[d, part].astype(F32) + recv[j, part].astype(F32)).astype(BF16)
                if j > 0:
                    push(
                        own.at[d, part], late.at[j - 1, part], ssem, rsem, where(-side * j)
                    )
        sent.append((own.at[pl.ds(0, 3)], ssem))

    def gather(own, late, rsem, base):
        settle(late, rsem)
        acc = own[base].astype(F32)
        for j in range(3):
            acc += late[j].astype(F32)
        return acc

    swap(a_own, a_recv, a_s, a_r, z, at_z)
    swap(b_own, b_recv, b_s, b_r, y, at_y)
    send_on(a_own, a_recv, a_r, a_late, al_s, al_r, z, at_z)
    send_on(b_own, b_recv, b_r, b_late, bl_s, bl_r, y, at_y)

    def total(own, recv, rsem, base):
        settle(recv.at[pl.ds(1, 7)], rsem)
        acc = own[base].astype(F32)
        for k in range(1, 8):
            acc += recv[k].astype(F32)
        return acc

    settle(in_nums.at[pl.ds(1, 15)], num_r)
    settle(in_rows.at[pl.ds(1, 15)], row_r)
    arrived = in_rows[...].reshape(256, 512)
    first, second = in_nums[0], in_nums[8]
    for k in range(1, 8):
        first += in_nums[k]
        second += in_nums[8 + k]
    named = jnp.concatenate([first, second], axis=1).astype(jnp.int32)
    place = iota((512, 256), 0)
    hot_z = jnp.where(place == named, 1.0, 0.0).astype(BF16)
    place = (place // 8 % 8) * 64 + (place // 64) * 8 + place % 8
    hot_y = jnp.where(place == named, 1.0, 0.0).astype(BF16)
    t1_own[...] = cells(mm(hot_z, arrived[:, 0:256]))
    t2_own[...] = cells(mm(hot_y, arrived[:, 256:512]))
    spread(t1_own, t1_recv, t1_s, t1_r, z, at_z)
    spread(t2_own, t2_recv, t2_s, t2_r, y, at_y)

    tall = jnp.transpose(total(o1_own, o1_recv, o1_r, x)).reshape(8, 4, 16, 32)
    o2_own[...] = jnp.concatenate([tall[:, g] for g in range(4)], axis=-1).astype(BF16)
    spread(o2_own, o2_recv, o2_s, o2_r, z, at_z)
    a2_own[...] = gather(a_own, a_late, al_r, z).astype(BF16)
    spread(a2_own, a2_recv, a2_s, a2_r, y, at_y)
    b2_own[...] = gather(b_own, b_late, bl_r, y).astype(BF16)
    spread(b2_own, b2_recv, b2_s, b2_r, z, at_z)

    t3_own[...] = total(t1_own, t1_recv, t1_r, z).astype(BF16)
    spread(t3_own, t3_recv, t3_s, t3_r, y, at_y)
    t4_own[...] = total(t2_own, t2_recv, t2_r, y).astype(BF16)
    spread(t4_own, t4_recv, t4_s, t4_r, z, at_z)

    o3_own[...] = total(o2_own, o2_recv, o2_r, z).astype(BF16)
    for k in far:
        push(o3_own, o3_recv.at[k], o3_s, o3_r, at_y(k))
    sent.append((o3_recv.at[pl.ds(0, 7)], o3_s))

    a_cell = total(a2_own, a2_recv, a2_r, y)
    b_cell = total(b2_own, b2_recv, b2_r, z)
    quarter = iota((8, 128), 1) // 32
    for xh, source_cell in ((0, a_cell), (1, b_cell)):
        for xl in range(4):
            acc = jnp.zeros((8, 128), F32)
            for g in range(4):
                piece = source_cell[8 * g:8 * g + 8]
                if g != xl:
                    piece = pltpu.roll(piece, 32 * ((g - xl) % 4), 1)
                acc = jnp.where(quarter == g, piece, acc)
            x_own[xh * 4 + xl] = acc
    spread(x_own, x_recv, x_s, x_r, x, at_x)

    left = total(t3_own, t3_recv, t3_r, y)
    right = total(t4_own, t4_recv, t4_r, z)
    touched_ref[:, 0:128] = left[0:8]
    touched_ref[:, 128:256] = left[8:16]
    touched_ref[:, 256:384] = right[0:8]
    touched_ref[:, 384:512] = right[8:16]

    settle(o3_recv.at[pl.ds(1, 7)], o3_r)
    flip[...] = o3_own[...].astype(F32)
    for k in range(1, 8):
        flip[...] += o3_recv[k].astype(F32)
    part = flip[pl.ds(pl.multiple_of(lax.rem(y, 2) * 8, 8), 8), :]
    acc = part
    for g in range(1, 4):
        acc = jnp.where(lax.div(y, 2) == g, pltpu.roll(part, 128 - 32 * g, 1), acc)
    last_ref[8:16, :] = acc
    last_ref[0:8, :] = total(x_own, x_recv, x_r, x)

    sent.append((er2.at[own_half], pair_s.at[0]))
    sent.append((nbf.at[0], pair_s.at[1]))
    sent.append((gtf.at[0], pair_s.at[2]))
    sent.append((d2.at[own_half], pair_s.at[3]))
    sent.append((out_rows.at[pl.ds(1, 15)], row_s))
    sent.append((out_nums.at[pl.ds(1, 15)], num_s))
    for ref, sem in sent:
        settle(ref, sem)


def finish(rows_ref, last_ref, touched_ref, gin_ref, gout_ref):
    touched_ref[...] = rows_ref[...]
    scale = 1.0 / math.sqrt(TOK * 16 * 64)
    tall = jnp.concatenate([last_ref[...] * scale, jnp.zeros((112, 128), F32)], axis=0)
    turned = jnp.transpose(tall)
    for g in range(4):
        gin_ref[:, 8 * g:8 * g + 8] = turned[32 * g:32 * g + 32, 0:8]
    gout_ref[...] = last_ref[8:16, 0:32] * scale


def on_device(tokens, cotangent, hist_len, item_owner, item_slot, w_in, w_out):
    vmem = pl.BlockSpec(memory_space=pltpu.VMEM)
    hbm = pl.BlockSpec(memory_space=pltpu.HBM)

    def buf(*shape, dtype=BF16):
        return pltpu.VMEM(shape, dtype)

    def sems(n):
        return pltpu.SemaphoreType.DMA((n,))

    rows, last = pl.pallas_call(
        kernel,
        out_shape=(
            jax.ShapeDtypeStruct((8, 512), F32),
            jax.ShapeDtypeStruct((16, 128), F32),
        ),
        in_specs=[hbm] * 7,
        out_specs=(vmem, vmem),
        scratch_shapes=[
            pltpu.SMEM((2,), jnp.int32), buf(TOK, D), buf(TOK, D),
            buf(1, TOK, dtype=jnp.int32), buf(1, TOK, dtype=jnp.int32),
            buf(512, 2048), buf(512, 512), buf(TOK, 2048, dtype=F32), buf(TOK, 2048),
            buf(256, 2048), buf(256, 256), buf(256, 256), buf(256, 512),
            buf(2, TOK, 256), buf(2, TOK, 256),
            buf(16, 16, 512), buf(16, 16, 512),
            buf(16, 1, 128, dtype=F32), buf(16, 1, 128, dtype=F32),
            buf(8, 8, 32, 128), buf(4, 8, 32, 128), buf(3, 8, 32, 128),
            buf(8, 8, 32, 128), buf(4, 8, 32, 128), buf(3, 8, 32, 128),
            buf(8, 8, 16, 128), buf(8, 8, 16, 128), buf(8, 8, 16, 128), buf(8, 8, 16, 128),
            buf(8, 32, 128), buf(8, 32, 128), buf(8, 32, 128), buf(8, 32, 128),
            buf(8, 16, 128), buf(8, 16, 128), buf(8, 16, 128), buf(8, 16, 128),
            buf(8, 8, 128, dtype=F32), buf(8, 8, 128, dtype=F32),
            buf(8, 32, 512), buf(8, 32, 512), buf(8, 16, 128), buf(8, 16, 128),
            buf(16, 128), buf(8, 16, 128), buf(16, 128, dtype=F32),
            sems(10), sems(4), sems(4),
        ] + [pltpu.SemaphoreType.DMA] * 32,
        compiler_params=pltpu.CompilerParams(
            collective_id=0, has_side_effects=True, vmem_limit_bytes=62 * 1024 * 1024
        ),
    )(
        hist_len, tokens, cotangent, item_owner.reshape(1, TOK), item_slot.reshape(1, TOK),
        w_in, w_out,
    )
    touched, grad_in, grad_out = pl.pallas_call(
        finish,
        out_shape=(
            jax.ShapeDtypeStruct((8, 512), F32),
            jax.ShapeDtypeStruct((32, 32), F32),
            jax.ShapeDtypeStruct((8, 32), F32),
        ),
        in_specs=[vmem, vmem],
        out_specs=(vmem, vmem, vmem),
        compiler_params=pltpu.CompilerParams(vmem_limit_bytes=62 * 1024 * 1024),
    )(rows, last)
    return touched, grad_in, grad_out.T


def solution(mesh):
    return jax.shard_map(
        on_device,
        mesh=mesh,
        in_specs=(
            P(("table", "rep"), None),
            P(("table", "rep"), None),
            P(("table", "rep")),
            P(("table", "rep"), None),
            P(("table", "rep")),
            P(),
            P(),
        ),
        out_specs=(P(("table", "rep"), None), P("table", "rep"), P("table", "rep")),
        check_vma=False,
    )
```

```python
import math

import jax
import jax.numpy as jnp
from jax import lax
from jax.experimental import pallas as pl
from jax.experimental.pallas import tpu as pltpu
from jax.sharding import PartitionSpec as P

D = 512
HEADS = 4
DH = 128
SLOTS_H = 64
TOK = 128
F32 = jnp.float32
BF16 = jnp.bfloat16
MESH = pl.DeviceIdType.MESH
NT = (((1,), (1,)), ((), ()))
TN = (((0,), (0,)), ((), ()))


def mm(a, b, dims=(((1,), (0,)), ((), ()))):
    return lax.dot_general(a, b, dims, preferred_element_type=F32)


def norm_rows(values):
    middle = jnp.mean(values, axis=-1, keepdims=True)
    centered = values - middle
    inverse = lax.rsqrt(jnp.mean(centered * centered, axis=-1, keepdims=True) + 1e-06)
    return centered * inverse, inverse


def norm_back(upstream, normed, inverse):
    first = jnp.mean(upstream, axis=-1, keepdims=True)
    second = jnp.mean(upstream * normed, axis=-1, keepdims=True)
    return inverse * (upstream - first - normed * second)


def sigmoid(values):
    return 0.5 * jnp.tanh(0.5 * values) + 0.5


def iota(shape, dim):
    return lax.broadcasted_iota(jnp.int32, shape, dim)


def cells(block):
    lo = block[:, :128].reshape(64, 8, 128)
    hi = block[:, 128:].reshape(64, 8, 128)
    return jnp.concatenate([lo, hi], axis=1).reshape(8, 8, 16, 128).astype(BF16)


def kernel(
    len_hbm, tok_hbm, cot_hbm, own_hbm, slot_hbm, w_in_hbm, w_out_hbm,
    touched_ref, last_ref,
    len_ref, tok_ref, cot_ref, own_ref, slot_ref, w_in, w_out, sgrad, hid, d2, nb2, gt2, er2, nbf, gtf,
    out_rows, in_rows, out_nums, in_nums, a_own, a_recv, a_late, b_own, b_recv, b_late,
    t1_own, t1_recv, t1_late, t2_own, t2_recv, t2_late,
    a2_own, a2_recv, b2_own, b2_recv, t3_own, t3_recv, t4_own, t4_recv,
    x_own, x_recv, o1_own, o1_recv, o2_own, o2_recv, o3_own, o3_recv, flip,
    w_sem, pair_s, pair_r, row_s, row_r, a_s, a_r, b_s, b_r,
    t1_s, t1_r, t2_s, t2_r, a2_s, a2_r, b2_s, b2_r, t3_s, t3_r, t4_s, t4_r, x_s, x_r,
    o1_s, o1_r, o2_s, o2_r, o3_s, o3_r, al_s, al_r, bl_s, bl_r, num_s, num_r,
    tl1_s, tl1_r, tl2_s, tl2_r,
):
    t = lax.axis_index("table")
    r = lax.axis_index("rep")
    x, core = lax.div(t, 2), lax.rem(t, 2)
    z, y = lax.div(r, 8), lax.rem(r, 8)

    def turn(base, k, n=8):
        return lax.rem(base + (k + n), n)

    def at_z(k):
        return (t, turn(z, k) * 8 + y)

    def at_y(k):
        return (t, z * 8 + turn(y, k))

    def at_t(k):
        return (turn(t, k, 16), r)

    def at_x(k):
        return (turn(x, k) * 2 + core, r)

    mate = (x * 2 + (1 - core), r)
    sent = []

    def push(src, dst, ssem, rsem, where):
        pltpu.make_async_remote_copy(
            src_ref=src, dst_ref=dst, send_sem=ssem, recv_sem=rsem,
            device_id=where, device_id_type=MESH,
        ).start()

    def settle(ref, sem):
        pltpu.make_async_copy(ref, ref, sem).wait()

    far = (4, 3, 5, 2, 6, 1, 7)

    def spread(own, recv, ssem, rsem, base, where):
        for k in far:
            push(own.at[turn(base, k)], recv.at[k], ssem, rsem, where(k))
        sent.append((own.at[pl.ds(0, 7)], ssem))

    small = []
    for n, (there, here) in enumerate((
        (tok_hbm, tok_ref), (len_hbm, len_ref), (cot_hbm, cot_ref), (own_hbm, own_ref), (slot_hbm, slot_ref),
    )):
        small.append(pltpu.make_async_copy(there, here, w_sem.at[5 + n]))
        small[-1].start()
    loads = []
    for b in range(4):
        cols = pl.ds(b * 512, 512)
        loads.append(pltpu.make_async_copy(w_in_hbm.at[:, cols], w_in.at[:, cols], w_sem.at[b]))
    loads.append(pltpu.make_async_copy(w_out_hbm, w_out, w_sem.at[4]))
    for load in loads:
        load.start()

    barrier = pltpu.get_barrier_semaphore()
    partners = [at_z(k) for k in range(1, 8)] + [at_y(k) for k in range(1, 8)]
    partners += [at_t(k) for k in range(1, 16)]
    for where in partners:
        pl.semaphore_signal(barrier, inc=1, device_id=where, device_id_type=MESH)

    small[1].wait()
    len0, len1 = len_ref[0], len_ref[1]
    ri, ci = iota((TOK, TOK), 0), iota((TOK, TOK), 1)
    same = (ri < SLOTS_H) == (ci < SLOTS_H)
    limit = jnp.where(ci < SLOTS_H, len0, len1 + SLOTS_H)
    keep = same & (ci <= ri) & (ci < limit)
    rows_i = iota((TOK, D), 0)
    valid = rows_i < jnp.where(rows_i < SLOTS_H, len0, len1 + SLOTS_H)

    small[0].wait()
    normed, inv_tok = norm_rows(tok_ref[...].astype(F32))
    nb = normed.astype(BF16)
    pi, pj = iota((D, D), 0), iota((D, D), 1)
    source = ((pj // 32) % 8) * 64 + (pj // 256) * 32 + pj % 32
    perm = jnp.where(pi == source, 1.0, 0.0).astype(BF16)
    nbp = mm(nb, perm).astype(BF16)
    nbf[0] = nbp[:, :256]
    nbf[1] = nbp[:, 256:]
    nb2[0:TOK, :] = nbf[core]
    small[2].wait()
    err = jnp.where(valid, cot_ref[...], jnp.zeros((TOK, D), BF16))
    er2[0:TOK, :] = err
    small[3].wait()
    small[4].wait()
    owner = own_ref[...]
    slot = slot_ref[...]
    ahead = lax.rem(owner - t + 16, 16)
    hot = jnp.where(iota((16, TOK), 0) == ahead, 1.0, 0.0)
    before = jnp.where(ri < ci, 1.0, 0.0).astype(BF16)
    earlier = mm(hot.astype(BF16), before)
    placed = jnp.sum(earlier * hot, axis=0, keepdims=True)
    key = ahead.astype(F32) * 16.0 + placed
    pick = jnp.where(iota((256, TOK), 0).astype(F32) == key, 1.0, 0.0)
    pick = pick.astype(BF16)
    line = lax.rem(ahead, 8).astype(F32) * 16.0 + placed
    spot = jnp.where(ri.astype(F32) == line, 1.0, 0.0).astype(BF16)
    high = mm((hot * (slot // 16).astype(F32)).astype(BF16), spot, NT)
    low = mm((hot * (slot % 16).astype(F32)).astype(BF16), spot, NT)
    numbers = high * 16.0 + low
    for k in range(16):
        out_nums[k] = numbers[k:k + 1, :]
    for b in range(4):
        cols = pl.ds(b * 512, 512)
        loads[b].wait()
        pre = mm(nb, w_in[:, cols])
        sig = sigmoid(pre)
        hid[:, cols] = (pre * sig).astype(BF16)
        sgrad[:, cols] = sig * (1.0 + pre * (1.0 - sig))
    pl.semaphore_wait(barrier, len(partners))
    own_half, mate_half = pl.ds(0, TOK), pl.ds(TOK, TOK)
    push(er2.at[own_half], er2.at[mate_half], pair_s.at[0], pair_r.at[0], mate)
    push(nbf.at[1 - core], nb2.at[mate_half], pair_s.at[1], pair_r.at[1], mate)
    score_scale = 1.0 / math.sqrt(DH)
    atts, slopes, mixes = [], [], []
    for h in range(HEADS):
        query = hid[:, 1024 + h * DH:1024 + (h + 1) * DH]
        keys = hid[:, 1536 + h * DH:1536 + (h + 1) * DH]
        vals = hid[:, 512 + h * DH:512 + (h + 1) * DH]
        score = mm(query, keys, NT) * score_scale
        sig = sigmoid(score)
        att = jnp.where(keep, score * sig * (1.0 / SLOTS_H), 0.0).astype(BF16)
        slopes.append(jnp.where(keep, sig * (1.0 + score * (1.0 - sig)) * (1.0 / SLOTS_H), 0.0))
        atts.append(att)
        mixes.append(mm(att, vals))
    on_mix, inv_mix = norm_rows(jnp.concatenate(mixes, axis=1))
    gate = hid[:, 0:512].astype(F32)
    gated = (on_mix * gate).astype(BF16)
    gtp = mm(gated, perm).astype(BF16)
    gtf[0] = gtp[:, :256]
    gtf[1] = gtp[:, 256:]
    gt2[0:TOK, :] = gtf[core]
    push(gtf.at[1 - core], gt2.at[mate_half], pair_s.at[2], pair_r.at[2], mate)

    loads[4].wait()
    dgate = mm(err, w_out[...], NT)

    def give(b, value):
        cols = pl.ds(b * 512, 512)
        d2[0:TOK, cols] = (value * sgrad[:, cols]).astype(BF16)
        push(d2.at[own_half, cols], d2.at[mate_half, cols], pair_s.at[3], pair_r.at[3], mate)

    give(0, dgate * on_mix)
    dmix = norm_back(dgate * gate, on_mix, inv_mix).astype(BF16)
    gv, gq, gk = [], [], []
    for h in range(HEADS):
        query = hid[:, 1024 + h * DH:1024 + (h + 1) * DH]
        keys = hid[:, 1536 + h * DH:1536 + (h + 1) * DH]
        vals = hid[:, 512 + h * DH:512 + (h + 1) * DH]
        part = dmix[:, h * DH:(h + 1) * DH]
        dscore = (mm(part, vals, NT) * slopes[h]).astype(BF16)
        gv.append(mm(atts[h], part, TN))
        gq.append(mm(dscore, keys) * score_scale)
        gk.append(mm(dscore, query, TN) * score_scale)
    give(1, jnp.concatenate(gv, axis=1))
    give(2, jnp.concatenate(gq, axis=1))
    give(3, jnp.concatenate(gk, axis=1))
    dnorm = mm(d2[0:TOK, 0:512], w_in[:, 0:512], NT)
    for b in range(1, 4):
        dnorm += mm(d2[0:TOK, b * 512:(b + 1) * 512], w_in[:, b * 512:(b + 1) * 512], NT)
    rows = (err.astype(F32) + norm_back(dnorm, normed, inv_tok)).astype(BF16)

    out_rows[...] = mm(pick, rows).astype(BF16).reshape(16, 16, 512)
    for k in (8, 7, 9, 6, 10, 5, 11, 4, 12, 3, 13, 2, 14, 1, 15):
        push(out_nums.at[k], in_nums.at[k], num_s, num_r, at_t(k))
        push(out_rows.at[k], in_rows.at[k], row_s, row_r, at_t(k))
    in_rows[0] = out_rows[0]
    in_nums[0] = out_nums[0]

    settle(er2.at[mate_half], pair_r.at[0])
    settle(nb2.at[mate_half], pair_r.at[1])
    settle(gt2.at[mate_half], pair_r.at[2])
    o1_own[...] = mm(gt2[...], er2[...], TN).astype(BF16).reshape(8, 32, 512)
    spread(o1_own, o1_recv, o1_s, o1_r, x, at_x)
    settle(d2.at[mate_half], pair_r.at[3])

    def block(k):
        d = turn(z, k)
        cols = pl.ds(pl.multiple_of(d * 256, 256), 256)
        part = mm(d2[:, cols], nb2[...], TN)
        a_own[d] = part[:, :128].reshape(8, 32, 128).astype(BF16)
        b_own[:, d] = part[:, 128:].reshape(8, 32, 128).astype(BF16)

    for k in (4, 3, -3, 2, -2, 1, -1, 0):
        block(k)

    def sides(base):
        side = 1 - 2 * lax.rem(base, 2)
        return ((pl.ds(0, 4), side), (pl.ds(4, 4), -side))

    def swap(own, recv, ssem, rsem, base, where):
        for j in (3, 2, 1, 0):
            for part, side in sides(base):
                push(
                    own.at[turn(base, side * (j + 1)), part], recv.at[j, part],
                    ssem, rsem, where(side),
                )
        sent.append((own.at[pl.ds(0, 4)], ssem))

    def send_on(own, recv, got, late, ssem, rsem, base, where):
        settle(recv, got)
        for j in (3, 2, 1, 0):
            for part, side in sides(base):
                d = turn(base, -side * j)
                own[d, part] = (own[d, part].astype(F32) + recv[j, part].astype(F32)).astype(BF16)
                if j > 0:
                    push(
                        own.at[d, part], late.at[j - 1, part], ssem, rsem, where(-side * j)
                    )
        sent.append((own.at[pl.ds(0, 3)], ssem))

    def gather(own, late, rsem, base):
        settle(late, rsem)
        acc = own[base].astype(F32)
        for j in range(3):
            acc += late[j].astype(F32)
        return acc

    swap(a_own, a_recv, a_s, a_r, z, at_z)
    swap(b_own, b_recv, b_s, b_r, y, at_y)
    send_on(a_own, a_recv, a_r, a_late, al_s, al_r, z, at_z)
    send_on(b_own, b_recv, b_r, b_late, bl_s, bl_r, y, at_y)

    def total(own, recv, rsem, base):
        settle(recv.at[pl.ds(1, 7)], rsem)
        acc = own[base].astype(F32)
        for k in range(1, 8):
            acc += recv[k].astype(F32)
        return acc

    settle(in_nums.at[pl.ds(1, 15)], num_r)
    settle(in_rows.at[pl.ds(1, 15)], row_r)
    arrived = in_rows[...].reshape(256, 512)
    first, second = in_nums[0], in_nums[8]
    for k in range(1, 8):
        first += in_nums[k]
        second += in_nums[8 + k]
    named = jnp.concatenate([first, second], axis=1).astype(jnp.int32)
    place = iota((512, 256), 0)
    hot_z = jnp.where(place == named, 1.0, 0.0).astype(BF16)
    place = (place // 8 % 8) * 64 + (place // 64) * 8 + place % 8
    hot_y = jnp.where(place == named, 1.0, 0.0).astype(BF16)
    t1_own[...] = cells(mm(hot_z, arrived[:, 0:256]))
    t2_own[...] = cells(mm(hot_y, arrived[:, 256:512]))
    swap(t1_own, t1_recv, t1_s, t1_r, z, at_z)
    swap(t2_own, t2_recv, t2_s, t2_r, y, at_y)

    a2_own[...] = gather(a_own, a_late, al_r, z).astype(BF16)
    spread(a2_own, a2_recv, a2_s, a2_r, y, at_y)
    b2_own[...] = gather(b_own, b_late, bl_r, y).astype(BF16)
    spread(b2_own, b2_recv, b2_s, b2_r, z, at_z)
    send_on(t1_own, t1_recv, t1_r, t1_late, tl1_s, tl1_r, z, at_z)
    send_on(t2_own, t2_recv, t2_r, t2_late, tl2_s, tl2_r, y, at_y)

    tall = jnp.transpose(total(o1_own, o1_recv, o1_r, x)).reshape(8, 4, 16, 32)
    o2_own[...] = jnp.concatenate([tall[:, g] for g in range(4)], axis=-1).astype(BF16)
    spread(o2_own, o2_recv, o2_s, o2_r, z, at_z)

    a_cell = total(a2_own, a2_recv, a2_r, y)
    b_cell = total(b2_own, b2_recv, b2_r, z)
    quarter = iota((8, 128), 1) // 32
    for xh, source_cell in ((0, a_cell), (1, b_cell)):
        for xl in range(4):
            acc = jnp.zeros((8, 128), F32)
            for g in range(4):
                piece = source_cell[8 * g:8 * g + 8]
                if g != xl:
                    piece = pltpu.roll(piece, 32 * ((g - xl) % 4), 1)
                acc = jnp.where(quarter == g, piece, acc)
            x_own[xh * 4 + xl] = acc
    spread(x_own, x_recv, x_s, x_r, x, at_x)

    t3_own[...] = gather(t1_own, t1_late, tl1_r, z).astype(BF16)
    spread(t3_own, t3_recv, t3_s, t3_r, y, at_y)
    t4_own[...] = gather(t2_own, t2_late, tl2_r, y).astype(BF16)
    spread(t4_own, t4_recv, t4_s, t4_r, z, at_z)

    o3_own[...] = total(o2_own, o2_recv, o2_r, z).astype(BF16)
    for k in far:
        push(o3_own, o3_recv.at[k], o3_s, o3_r, at_y(k))
    sent.append((o3_recv.at[pl.ds(0, 7)], o3_s))

    last_ref[0:8, :] = total(x_own, x_recv, x_r, x)
    left = total(t3_own, t3_recv, t3_r, y)
    right = total(t4_own, t4_recv, t4_r, z)
    touched_ref[:, 0:128] = left[0:8]
    touched_ref[:, 128:256] = left[8:16]
    touched_ref[:, 256:384] = right[0:8]
    touched_ref[:, 384:512] = right[8:16]

    settle(o3_recv.at[pl.ds(1, 7)], o3_r)
    flip[...] = o3_own[...].astype(F32)
    for k in range(1, 8):
        flip[...] += o3_recv[k].astype(F32)
    part = flip[pl.ds(pl.multiple_of(lax.rem(y, 2) * 8, 8), 8), :]
    acc = part
    for g in range(1, 4):
        acc = jnp.where(lax.div(y, 2) == g, pltpu.roll(part, 128 - 32 * g, 1), acc)
    last_ref[8:16, :] = acc

    sent.append((er2.at[own_half], pair_s.at[0]))
    sent.append((nbf.at[0], pair_s.at[1]))
    sent.append((gtf.at[0], pair_s.at[2]))
    sent.append((d2.at[own_half], pair_s.at[3]))
    sent.append((out_rows.at[pl.ds(1, 15)], row_s))
    sent.append((out_nums.at[pl.ds(1, 15)], num_s))
    for ref, sem in sent:
        settle(ref, sem)


def finish(rows_ref, last_ref, touched_ref, gin_ref, gout_ref):
    touched_ref[...] = rows_ref[...]
    scale = 1.0 / math.sqrt(TOK * 16 * 64)
    tall = jnp.concatenate([last_ref[...] * scale, jnp.zeros((112, 128), F32)], axis=0)
    turned = jnp.transpose(tall)
    for g in range(4):
        gin_ref[:, 8 * g:8 * g + 8] = turned[32 * g:32 * g + 32, 0:8]
    gout_ref[...] = last_ref[8:16, 0:32] * scale


def on_device(tokens, cotangent, hist_len, item_owner, item_slot, w_in, w_out):
    vmem = pl.BlockSpec(memory_space=pltpu.VMEM)
    hbm = pl.BlockSpec(memory_space=pltpu.HBM)

    def buf(*shape, dtype=BF16):
        return pltpu.VMEM(shape, dtype)

    def sems(n):
        return pltpu.SemaphoreType.DMA((n,))

    rows, last = pl.pallas_call(
        kernel,
        out_shape=(
            jax.ShapeDtypeStruct((8, 512), F32),
            jax.ShapeDtypeStruct((16, 128), F32),
        ),
        in_specs=[hbm] * 7,
        out_specs=(vmem, vmem),
        scratch_shapes=[
            pltpu.SMEM((2,), jnp.int32), buf(TOK, D), buf(TOK, D),
            buf(1, TOK, dtype=jnp.int32), buf(1, TOK, dtype=jnp.int32),
            buf(512, 2048), buf(512, 512), buf(TOK, 2048, dtype=F32), buf(TOK, 2048),
            buf(256, 2048), buf(256, 256), buf(256, 256), buf(256, 512),
            buf(2, TOK, 256), buf(2, TOK, 256),
            buf(16, 16, 512), buf(16, 16, 512),
            buf(16, 1, 128, dtype=F32), buf(16, 1, 128, dtype=F32),
            buf(8, 8, 32, 128), buf(4, 8, 32, 128), buf(3, 8, 32, 128),
            buf(8, 8, 32, 128), buf(4, 8, 32, 128), buf(3, 8, 32, 128),
            buf(8, 8, 16, 128), buf(4, 8, 16, 128), buf(3, 8, 16, 128),
            buf(8, 8, 16, 128), buf(4, 8, 16, 128), buf(3, 8, 16, 128),
            buf(8, 32, 128), buf(8, 32, 128), buf(8, 32, 128), buf(8, 32, 128),
            buf(8, 16, 128), buf(8, 16, 128), buf(8, 16, 128), buf(8, 16, 128),
            buf(8, 8, 128, dtype=F32), buf(8, 8, 128, dtype=F32),
            buf(8, 32, 512), buf(8, 32, 512), buf(8, 16, 128), buf(8, 16, 128),
            buf(16, 128), buf(8, 16, 128), buf(16, 128, dtype=F32),
            sems(10), sems(4), sems(4),
        ] + [pltpu.SemaphoreType.DMA] * 36,
        compiler_params=pltpu.CompilerParams(
            collective_id=0, has_side_effects=True, vmem_limit_bytes=62 * 1024 * 1024
        ),
    )(
        hist_len, tokens, cotangent, item_owner.reshape(1, TOK), item_slot.reshape(1, TOK),
        w_in, w_out,
    )
    touched, grad_in, grad_out = pl.pallas_call(
        finish,
        out_shape=(
            jax.ShapeDtypeStruct((8, 512), F32),
            jax.ShapeDtypeStruct((32, 32), F32),
            jax.ShapeDtypeStruct((8, 32), F32),
        ),
        in_specs=[vmem, vmem],
        out_specs=(vmem, vmem, vmem),
        compiler_params=pltpu.CompilerParams(vmem_limit_bytes=62 * 1024 * 1024),
    )(rows, last)
    return touched, grad_in, grad_out.T


def solution(mesh):
    return jax.shard_map(
        on_device,
        mesh=mesh,
        in_specs=(
            P(("table", "rep"), None),
            P(("table", "rep"), None),
            P(("table", "rep")),
            P(("table", "rep"), None),
            P(("table", "rep")),
            P(),
            P(),
        ),
        out_specs=(P(("table", "rep"), None), P("table", "rep"), P("table", "rep")),
        check_vma=False,
    )
```

```python
import math

import jax
import jax.numpy as jnp
from jax import lax
from jax.experimental import pallas as pl
from jax.experimental.pallas import tpu as pltpu
from jax.sharding import PartitionSpec as P

D = 512
HEADS = 4
DH = 128
SLOTS_H = 64
TOK = 128
F32 = jnp.float32
BF16 = jnp.bfloat16
MESH = pl.DeviceIdType.MESH
NT = (((1,), (1,)), ((), ()))
TN = (((0,), (0,)), ((), ()))


def mm(a, b, dims=(((1,), (0,)), ((), ()))):
    return lax.dot_general(a, b, dims, preferred_element_type=F32)


def norm_rows(values):
    middle = jnp.mean(values, axis=-1, keepdims=True)
    centered = values - middle
    inverse = lax.rsqrt(jnp.mean(centered * centered, axis=-1, keepdims=True) + 1e-06)
    return centered * inverse, inverse


def norm_back(upstream, normed, inverse):
    first = jnp.mean(upstream, axis=-1, keepdims=True)
    second = jnp.mean(upstream * normed, axis=-1, keepdims=True)
    return inverse * (upstream - first - normed * second)


def sigmoid(values):
    return 0.5 * jnp.tanh(0.5 * values) + 0.5


def iota(shape, dim):
    return lax.broadcasted_iota(jnp.int32, shape, dim)


def cells(block):
    lo = block[:, :128].reshape(64, 8, 128)
    hi = block[:, 128:].reshape(64, 8, 128)
    return jnp.concatenate([lo, hi], axis=1).reshape(8, 8, 16, 128).astype(BF16)


def kernel(
    len_hbm, tok_hbm, cot_hbm, own_hbm, slot_hbm, w_in_hbm, w_out_hbm,
    touched_ref, last_ref,
    len_ref, tok_ref, cot_ref, own_ref, slot_ref, w_in, w_out, sgrad, hid, d2, nb2, gt2, er2, nbf, gtf,
    out_rows, in_rows, out_nums, in_nums, a_own, a_recv, a_late, b_own, b_recv, b_late,
    t1_own, t1_recv, t1_late, t2_own, t2_recv, t2_late,
    a2_own, a2_recv, b2_own, b2_recv, t3_own, t3_recv, t4_own, t4_recv,
    x_own, x_recv, o1_own, o1_recv, o2_own, o2_recv, o3_own, o3_recv, flip,
    w_sem, pair_s, pair_r, row_s, row_r, a_s, a_r, b_s, b_r,
    t1_s, t1_r, t2_s, t2_r, a2_s, a2_r, b2_s, b2_r, t3_s, t3_r, t4_s, t4_r, x_s, x_r,
    o1_s, o1_r, o2_s, o2_r, o3_s, o3_r, al_s, al_r, bl_s, bl_r, num_s, num_r,
    tl1_s, tl1_r, tl2_s, tl2_r,
):
    t = lax.axis_index("table")
    r = lax.axis_index("rep")
    x, core = lax.div(t, 2), lax.rem(t, 2)
    z, y = lax.div(r, 8), lax.rem(r, 8)

    def turn(base, k, n=8):
        return lax.rem(base + (k + n), n)

    def at_z(k):
        return (t, turn(z, k) * 8 + y)

    def at_y(k):
        return (t, z * 8 + turn(y, k))

    def at_t(k):
        return (turn(t, k, 16), r)

    def at_x(k):
        return (turn(x, k) * 2 + core, r)

    mate = (x * 2 + (1 - core), r)
    sent = []

    def push(src, dst, ssem, rsem, where):
        pltpu.make_async_remote_copy(
            src_ref=src, dst_ref=dst, send_sem=ssem, recv_sem=rsem,
            device_id=where, device_id_type=MESH,
        ).start()

    def settle(ref, sem):
        pltpu.make_async_copy(ref, ref, sem).wait()

    far = (4, 3, 5, 2, 6, 1, 7)

    def spread(own, recv, ssem, rsem, base, where):
        for k in far:
            push(own.at[turn(base, k)], recv.at[k], ssem, rsem, where(k))
        sent.append((own.at[pl.ds(0, 7)], ssem))

    small = []
    for n, (there, here) in enumerate((
        (tok_hbm, tok_ref), (len_hbm, len_ref), (cot_hbm, cot_ref), (own_hbm, own_ref), (slot_hbm, slot_ref),
    )):
        small.append(pltpu.make_async_copy(there, here, w_sem.at[5 + n]))
        small[-1].start()
    loads = []
    for b in range(4):
        cols = pl.ds(b * 512, 512)
        loads.append(pltpu.make_async_copy(w_in_hbm.at[:, cols], w_in.at[:, cols], w_sem.at[b]))
    loads.append(pltpu.make_async_copy(w_out_hbm, w_out, w_sem.at[4]))
    for load in loads:
        load.start()

    barrier = pltpu.get_barrier_semaphore()
    partners = [at_z(k) for k in range(1, 8)] + [at_y(k) for k in range(1, 8)]
    partners += [at_t(k) for k in range(1, 16)]
    for where in partners:
        pl.semaphore_signal(barrier, inc=1, device_id=where, device_id_type=MESH)

    small[1].wait()
    len0, len1 = len_ref[0], len_ref[1]
    ri, ci = iota((TOK, TOK), 0), iota((TOK, TOK), 1)
    same = (ri < SLOTS_H) == (ci < SLOTS_H)
    limit = jnp.where(ci < SLOTS_H, len0, len1 + SLOTS_H)
    keep = same & (ci <= ri) & (ci < limit)
    rows_i = iota((TOK, D), 0)
    valid = rows_i < jnp.where(rows_i < SLOTS_H, len0, len1 + SLOTS_H)

    small[0].wait()
    normed, inv_tok = norm_rows(tok_ref[...].astype(F32))
    nb = normed.astype(BF16)
    pi, pj = iota((D, D), 0), iota((D, D), 1)
    source = ((pj // 32) % 8) * 64 + (pj // 256) * 32 + pj % 32
    perm = jnp.where(pi == source, 1.0, 0.0).astype(BF16)
    nbp = mm(nb, perm).astype(BF16)
    nbf[0] = nbp[:, :256]
    nbf[1] = nbp[:, 256:]
    nb2[0:TOK, :] = nbf[core]
    small[2].wait()
    err = jnp.where(valid, cot_ref[...], jnp.zeros((TOK, D), BF16))
    er2[0:TOK, :] = err
    small[3].wait()
    small[4].wait()
    owner = own_ref[...]
    slot = slot_ref[...]
    ahead = lax.rem(owner - t + 16, 16)
    hot = jnp.where(iota((16, TOK), 0) == ahead, 1.0, 0.0)
    before = jnp.where(ri < ci, 1.0, 0.0).astype(BF16)
    earlier = mm(hot.astype(BF16), before)
    placed = jnp.sum(earlier * hot, axis=0, keepdims=True)
    key = ahead.astype(F32) * 16.0 + placed
    pick = jnp.where(iota((256, TOK), 0).astype(F32) == key, 1.0, 0.0)
    pick = pick.astype(BF16)
    line = lax.rem(ahead, 8).astype(F32) * 16.0 + placed
    spot = jnp.where(ri.astype(F32) == line, 1.0, 0.0).astype(BF16)
    high = mm((hot * (slot // 16).astype(F32)).astype(BF16), spot, NT)
    low = mm((hot * (slot % 16).astype(F32)).astype(BF16), spot, NT)
    numbers = high * 16.0 + low
    for k in range(16):
        out_nums[k] = numbers[k:k + 1, :]
    for b in range(4):
        cols = pl.ds(b * 512, 512)
        loads[b].wait()
        pre = mm(nb, w_in[:, cols])
        sig = sigmoid(pre)
        hid[:, cols] = (pre * sig).astype(BF16)
        sgrad[:, cols] = sig * (1.0 + pre * (1.0 - sig))
    pl.semaphore_wait(barrier, len(partners))
    own_half, mate_half = pl.ds(0, TOK), pl.ds(TOK, TOK)
    push(er2.at[own_half], er2.at[mate_half], pair_s.at[0], pair_r.at[0], mate)
    push(nbf.at[1 - core], nb2.at[mate_half], pair_s.at[1], pair_r.at[1], mate)
    score_scale = 1.0 / math.sqrt(DH)
    atts, slopes, mixes = [], [], []
    for h in range(HEADS):
        query = hid[:, 1024 + h * DH:1024 + (h + 1) * DH]
        keys = hid[:, 1536 + h * DH:1536 + (h + 1) * DH]
        vals = hid[:, 512 + h * DH:512 + (h + 1) * DH]
        score = mm(query, keys, NT) * score_scale
        sig = sigmoid(score)
        att = jnp.where(keep, score * sig * (1.0 / SLOTS_H), 0.0).astype(BF16)
        slopes.append(jnp.where(keep, sig * (1.0 + score * (1.0 - sig)) * (1.0 / SLOTS_H), 0.0))
        atts.append(att)
        mixes.append(mm(att, vals))
    on_mix, inv_mix = norm_rows(jnp.concatenate(mixes, axis=1))
    gate = hid[:, 0:512].astype(F32)
    gated = (on_mix * gate).astype(BF16)
    gtp = mm(gated, perm).astype(BF16)
    gtf[0] = gtp[:, :256]
    gtf[1] = gtp[:, 256:]
    gt2[0:TOK, :] = gtf[core]
    push(gtf.at[1 - core], gt2.at[mate_half], pair_s.at[2], pair_r.at[2], mate)

    loads[4].wait()
    dgate = mm(err, w_out[...], NT)

    def give(b, value):
        cols = pl.ds(b * 512, 512)
        d2[0:TOK, cols] = (value * sgrad[:, cols]).astype(BF16)
        push(d2.at[own_half, cols], d2.at[mate_half, cols], pair_s.at[3], pair_r.at[3], mate)

    give(0, dgate * on_mix)
    dmix = norm_back(dgate * gate, on_mix, inv_mix).astype(BF16)
    gv, gq, gk = [], [], []
    for h in range(HEADS):
        query = hid[:, 1024 + h * DH:1024 + (h + 1) * DH]
        keys = hid[:, 1536 + h * DH:1536 + (h + 1) * DH]
        vals = hid[:, 512 + h * DH:512 + (h + 1) * DH]
        part = dmix[:, h * DH:(h + 1) * DH]
        dscore = (mm(part, vals, NT) * slopes[h]).astype(BF16)
        gv.append(mm(atts[h], part, TN))
        gq.append(mm(dscore, keys) * score_scale)
        gk.append(mm(dscore, query, TN) * score_scale)
    give(1, jnp.concatenate(gv, axis=1))
    give(2, jnp.concatenate(gq, axis=1))
    give(3, jnp.concatenate(gk, axis=1))
    dnorm = mm(d2[0:TOK, 0:512], w_in[:, 0:512], NT)
    for b in range(1, 4):
        dnorm += mm(d2[0:TOK, b * 512:(b + 1) * 512], w_in[:, b * 512:(b + 1) * 512], NT)
    rows = (err.astype(F32) + norm_back(dnorm, normed, inv_tok)).astype(BF16)

    out_rows[...] = mm(pick, rows).astype(BF16).reshape(16, 16, 512)
    for k in (8, 7, 9, 6, 10, 5, 11, 4, 12, 3, 13, 2, 14, 1, 15):
        push(out_nums.at[k], in_nums.at[k], num_s, num_r, at_t(k))
        push(out_rows.at[k], in_rows.at[k], row_s, row_r, at_t(k))
    in_rows[0] = out_rows[0]
    in_nums[0] = out_nums[0]

    settle(er2.at[mate_half], pair_r.at[0])
    settle(nb2.at[mate_half], pair_r.at[1])
    settle(gt2.at[mate_half], pair_r.at[2])
    o1_own[...] = mm(gt2[...], er2[...], TN).astype(BF16).reshape(8, 32, 512)
    spread(o1_own, o1_recv, o1_s, o1_r, x, at_x)
    settle(d2.at[mate_half], pair_r.at[3])

    def block(k):
        d = turn(z, k)
        cols = pl.ds(pl.multiple_of(d * 256, 256), 256)
        part = mm(d2[:, cols], nb2[...], TN)
        a_own[d] = part[:, :128].reshape(8, 32, 128).astype(BF16)
        b_own[:, d] = part[:, 128:].reshape(8, 32, 128).astype(BF16)

    def sides(base):
        side = 1 - 2 * lax.rem(base, 2)
        return ((pl.ds(0, 4), side), (pl.ds(4, 4), -side))

    def swap_step(own, recv, ssem, rsem, base, where, j):
        for part, side in sides(base):
            push(
                own.at[turn(base, side * (j + 1)), part], recv.at[j, part],
                ssem, rsem, where(side),
            )

    def swap(own, recv, ssem, rsem, base, where):
        for j in (3, 2, 1, 0):
            swap_step(own, recv, ssem, rsem, base, where, j)
        sent.append((own.at[pl.ds(0, 4)], ssem))

    def send_on(own, recv, got, late, ssem, rsem, base, where):
        settle(recv, got)
        for j in (3, 2, 1, 0):
            for part, side in sides(base):
                d = turn(base, -side * j)
                own[d, part] = (own[d, part].astype(F32) + recv[j, part].astype(F32)).astype(BF16)
                if j > 0:
                    push(
                        own.at[d, part], late.at[j - 1, part], ssem, rsem, where(-side * j)
                    )
        sent.append((own.at[pl.ds(0, 3)], ssem))

    def gather(own, late, rsem, base):
        settle(late, rsem)
        acc = own[base].astype(F32)
        for j in range(3):
            acc += late[j].astype(F32)
        return acc

    for j, made in ((3, (4,)), (2, (3, -3)), (1, (2, -2)), (0, (1, -1))):
        for k in made:
            block(k)
        swap_step(a_own, a_recv, a_s, a_r, z, at_z, j)
    sent.append((a_own.at[pl.ds(0, 4)], a_s))
    block(0)
    swap(b_own, b_recv, b_s, b_r, y, at_y)
    send_on(a_own, a_recv, a_r, a_late, al_s, al_r, z, at_z)
    send_on(b_own, b_recv, b_r, b_late, bl_s, bl_r, y, at_y)

    def total(own, recv, rsem, base):
        settle(recv.at[pl.ds(1, 7)], rsem)
        acc = own[base].astype(F32)
        for k in range(1, 8):
            acc += recv[k].astype(F32)
        return acc

    settle(in_nums.at[pl.ds(1, 15)], num_r)
    settle(in_rows.at[pl.ds(1, 15)], row_r)
    arrived = in_rows[...].reshape(256, 512)
    first, second = in_nums[0], in_nums[8]
    for k in range(1, 8):
        first += in_nums[k]
        second += in_nums[8 + k]
    named = jnp.concatenate([first, second], axis=1).astype(jnp.int32)
    place = iota((512, 256), 0)
    hot_z = jnp.where(place == named, 1.0, 0.0).astype(BF16)
    t1_own[...] = cells(mm(hot_z, arrived[:, 0:256]))
    swap(t1_own, t1_recv, t1_s, t1_r, z, at_z)
    place = (place // 8 % 8) * 64 + (place // 64) * 8 + place % 8
    hot_y = jnp.where(place == named, 1.0, 0.0).astype(BF16)
    t2_own[...] = cells(mm(hot_y, arrived[:, 256:512]))
    swap(t2_own, t2_recv, t2_s, t2_r, y, at_y)

    a2_own[...] = gather(a_own, a_late, al_r, z).astype(BF16)
    spread(a2_own, a2_recv, a2_s, a2_r, y, at_y)
    b2_own[...] = gather(b_own, b_late, bl_r, y).astype(BF16)
    spread(b2_own, b2_recv, b2_s, b2_r, z, at_z)
    send_on(t1_own, t1_recv, t1_r, t1_late, tl1_s, tl1_r, z, at_z)
    send_on(t2_own, t2_recv, t2_r, t2_late, tl2_s, tl2_r, y, at_y)

    tall = jnp.transpose(total(o1_own, o1_recv, o1_r, x)).reshape(8, 4, 16, 32)
    o2_own[...] = jnp.concatenate([tall[:, g] for g in range(4)], axis=-1).astype(BF16)
    spread(o2_own, o2_recv, o2_s, o2_r, z, at_z)

    a_cell = total(a2_own, a2_recv, a2_r, y)
    b_cell = total(b2_own, b2_recv, b2_r, z)
    quarter = iota((8, 128), 1) // 32
    for xh, source_cell in ((0, a_cell), (1, b_cell)):
        for xl in range(4):
            acc = jnp.zeros((8, 128), F32)
            for g in range(4):
                piece = source_cell[8 * g:8 * g + 8]
                if g != xl:
                    piece = pltpu.roll(piece, 32 * ((g - xl) % 4), 1)
                acc = jnp.where(quarter == g, piece, acc)
            x_own[xh * 4 + xl] = acc
    spread(x_own, x_recv, x_s, x_r, x, at_x)

    t3_own[...] = gather(t1_own, t1_late, tl1_r, z).astype(BF16)
    spread(t3_own, t3_recv, t3_s, t3_r, y, at_y)
    t4_own[...] = gather(t2_own, t2_late, tl2_r, y).astype(BF16)
    spread(t4_own, t4_recv, t4_s, t4_r, z, at_z)

    o3_own[...] = total(o2_own, o2_recv, o2_r, z).astype(BF16)
    for k in far:
        push(o3_own, o3_recv.at[k], o3_s, o3_r, at_y(k))
    sent.append((o3_recv.at[pl.ds(0, 7)], o3_s))

    last_ref[0:8, :] = total(x_own, x_recv, x_r, x)
    left = total(t3_own, t3_recv, t3_r, y)
    right = total(t4_own, t4_recv, t4_r, z)
    touched_ref[:, 0:128] = left[0:8]
    touched_ref[:, 128:256] = left[8:16]
    touched_ref[:, 256:384] = right[0:8]
    touched_ref[:, 384:512] = right[8:16]

    settle(o3_recv.at[pl.ds(1, 7)], o3_r)
    flip[...] = o3_own[...].astype(F32)
    for k in range(1, 8):
        flip[...] += o3_recv[k].astype(F32)
    part = flip[pl.ds(pl.multiple_of(lax.rem(y, 2) * 8, 8), 8), :]
    acc = part
    for g in range(1, 4):
        acc = jnp.where(lax.div(y, 2) == g, pltpu.roll(part, 128 - 32 * g, 1), acc)
    last_ref[8:16, :] = acc

    sent.append((er2.at[own_half], pair_s.at[0]))
    sent.append((nbf.at[0], pair_s.at[1]))
    sent.append((gtf.at[0], pair_s.at[2]))
    sent.append((d2.at[own_half], pair_s.at[3]))
    sent.append((out_rows.at[pl.ds(1, 15)], row_s))
    sent.append((out_nums.at[pl.ds(1, 15)], num_s))
    for ref, sem in sent:
        settle(ref, sem)


def finish(rows_ref, last_ref, touched_ref, gin_ref, gout_ref):
    touched_ref[...] = rows_ref[...]
    scale = 1.0 / math.sqrt(TOK * 16 * 64)
    tall = jnp.concatenate([last_ref[...] * scale, jnp.zeros((112, 128), F32)], axis=0)
    turned = jnp.transpose(tall)
    for g in range(4):
        gin_ref[:, 8 * g:8 * g + 8] = turned[32 * g:32 * g + 32, 0:8]
    gout_ref[...] = last_ref[8:16, 0:32] * scale


def on_device(tokens, cotangent, hist_len, item_owner, item_slot, w_in, w_out):
    vmem = pl.BlockSpec(memory_space=pltpu.VMEM)
    hbm = pl.BlockSpec(memory_space=pltpu.HBM)

    def buf(*shape, dtype=BF16):
        return pltpu.VMEM(shape, dtype)

    def sems(n):
        return pltpu.SemaphoreType.DMA((n,))

    rows, last = pl.pallas_call(
        kernel,
        out_shape=(
            jax.ShapeDtypeStruct((8, 512), F32),
            jax.ShapeDtypeStruct((16, 128), F32),
        ),
        in_specs=[hbm] * 7,
        out_specs=(vmem, vmem),
        scratch_shapes=[
            pltpu.SMEM((2,), jnp.int32), buf(TOK, D), buf(TOK, D),
            buf(1, TOK, dtype=jnp.int32), buf(1, TOK, dtype=jnp.int32),
            buf(512, 2048), buf(512, 512), buf(TOK, 2048, dtype=F32), buf(TOK, 2048),
            buf(256, 2048), buf(256, 256), buf(256, 256), buf(256, 512),
            buf(2, TOK, 256), buf(2, TOK, 256),
            buf(16, 16, 512), buf(16, 16, 512),
            buf(16, 1, 128, dtype=F32), buf(16, 1, 128, dtype=F32),
            buf(8, 8, 32, 128), buf(4, 8, 32, 128), buf(3, 8, 32, 128),
            buf(8, 8, 32, 128), buf(4, 8, 32, 128), buf(3, 8, 32, 128),
            buf(8, 8, 16, 128), buf(4, 8, 16, 128), buf(3, 8, 16, 128),
            buf(8, 8, 16, 128), buf(4, 8, 16, 128), buf(3, 8, 16, 128),
            buf(8, 32, 128), buf(8, 32, 128), buf(8, 32, 128), buf(8, 32, 128),
            buf(8, 16, 128), buf(8, 16, 128), buf(8, 16, 128), buf(8, 16, 128),
            buf(8, 8, 128, dtype=F32), buf(8, 8, 128, dtype=F32),
            buf(8, 32, 512), buf(8, 32, 512), buf(8, 16, 128), buf(8, 16, 128),
            buf(16, 128), buf(8, 16, 128), buf(16, 128, dtype=F32),
            sems(10), sems(4), sems(4),
        ] + [pltpu.SemaphoreType.DMA] * 36,
        compiler_params=pltpu.CompilerParams(
            collective_id=0, has_side_effects=True, vmem_limit_bytes=62 * 1024 * 1024
        ),
    )(
        hist_len, tokens, cotangent, item_owner.reshape(1, TOK), item_slot.reshape(1, TOK),
        w_in, w_out,
    )
    touched, grad_in, grad_out = pl.pallas_call(
        finish,
        out_shape=(
            jax.ShapeDtypeStruct((8, 512), F32),
            jax.ShapeDtypeStruct((32, 32), F32),
            jax.ShapeDtypeStruct((8, 32), F32),
        ),
        in_specs=[vmem, vmem],
        out_specs=(vmem, vmem, vmem),
        compiler_params=pltpu.CompilerParams(vmem_limit_bytes=62 * 1024 * 1024),
    )(rows, last)
    return touched, grad_in, grad_out.T


def solution(mesh):
    return jax.shard_map(
        on_device,
        mesh=mesh,
        in_specs=(
            P(("table", "rep"), None),
            P(("table", "rep"), None),
            P(("table", "rep")),
            P(("table", "rep"), None),
            P(("table", "rep")),
            P(),
            P(),
        ),
        out_specs=(P(("table", "rep"), None), P("table", "rep"), P("table", "rep")),
        check_vma=False,
    )
```
